32 devices in a mesh: row: 8 (over z, core), col: 4 (over y, x).
Axes of the slice: x: 2, y: 2, z: 4, core: 2. Of those that a mesh axis runs over, the one named last changes fastest.
Arguments:
- panels: bfloat16 [256, 32, 256], P(('row', 'col')), may hold values from -21 to 21
- tiles: bfloat16 [1536, 256, 512], P(('row', 'col')), may hold values from -0.109375 to 0.109375
- tile_dst: int32 [1536], P(('row', 'col')), may hold values from 0 to 7
- tile_src: int32 [1536], P(('row', 'col')), may hold values from 0 to 63
- geometry: float32 [256, 6, 256], P(('row', 'col')), may hold values from -5 to 5
- areas: float32 [256, 256], P(('row', 'col')), may hold values from 0.25 to 2
- block_owner: int32 [256, 1], P(('row', 'col')), may hold values from 0 to 3; in each aligned block of 8 rows (0 to 7, 8 to 15, ...) at most 2 rows name the same one
- block_slot: int32 [256], P(('row', 'col')), may hold values from 0 to 3
Outputs:
- field: float32 [256, 32, 256], P(('row', 'col'))
- shape_gradient: float32 [256, 256], P(('row', 'col'))
The draws below stay inside these ranges and needn't reach their ends.
Inputs may be any that keep to these rules, and one draw needn't show every extreme that they name: Among the blocks of one device at most 2 have the same block_owner, and some device reaches 2.
All inputs are finite; a program needn't handle non-finite values.
Results may differ from the reference program's by a relative error of at most 0.0003.
Values may be sent and summed in bfloat16 or wider, within the bound.
No kernel may reach another device: no remote copies, remote signals or barrier semaphores. Data moves between devices by JAX's collectives and lax.ppermute only.
A program may use at most 64 MiB of HBM per device.

```python
import math
import jax
import jax.numpy as jnp
import numpy as np
from jax import lax

BN = 256
NF = 16
CAP = 2
NBD = 8
TPD = 48
PD = 4
NB = 256
NT = 1536
N_ROW = 8
N_COL = 4


def draw_panels(key, part):
    key_levels = jax.random.fold_in(key, 11)
    key_values = jax.random.fold_in(key, 12)
    levels = jnp.exp(jax.random.uniform(key_levels, (NF,), jnp.float32, math.log(0.3), math.log(3.0)))
    values = jnp.clip(jax.random.normal(key_values, (NB, 2, NF, BN), jnp.float32), -4.0, 4.0)
    scaled = values * levels[None, None, :, None]
    return scaled.reshape(NB, 2 * NF, BN).astype(jnp.bfloat16)


def with_ends(values, stream_key, smallest, largest):
    shape = values.shape
    spot = [jax.random.randint(jax.random.fold_in(stream_key, axis), (), 0, shape[axis]) for axis in range(len(shape))]
    values = values.at[tuple(spot)].set(smallest)
    longest = shape.index(max(shape))
    spot[longest] = (spot[longest] + 1) % shape[longest]
    return values.at[tuple(spot)].set(largest)


def steps_of(stream_key, extent, cuts, smallest, largest):
    loudness = 1.0
    for position, parts in cuts:
        steps = jax.random.uniform(jax.random.fold_in(jax.random.fold_in(stream_key, 6), position), (parts,), jnp.float32, smallest / len(cuts), largest / len(cuts))
        loudness = loudness * jnp.repeat(jnp.exp(steps), extent[position] // parts).reshape((-1,) + (1,) * (len(extent) - 1 - position))
    return loudness


def assign_block(rng, own, number, rows, amount, top, limit, skew):
    ranking = jax.random.permutation(rng, amount)
    crowded, usual = portions_of(amount, rows * top, limit, skew, True), portions_of(amount, rows * top, limit, skew, False)
    places = jnp.arange(amount)

    def named(lengths, rotation):
        used = int((lengths > 0).sum())
        fixed = max(1, used // 4)
        moved = fixed + (places - fixed + rotation * (used - fixed)) % max(1, amount - fixed)
        return jnp.zeros((amount,), jnp.int32).at[ranking[jnp.where(places < fixed, places, moved)]].set(jnp.asarray(lengths, jnp.int32))

    lengths = jnp.where(number % 4 == 0, named(crowded, number // 4), named(usual, number - number // 4 - 1))
    mixed = jax.random.permutation(jax.random.fold_in(own, 3), amount)
    donor, receiver = mixed[0:amount // 2 * 2:2], mixed[1:amount // 2 * 2:2]
    margin = jnp.minimum(lengths[donor] - 1, limit - lengths[receiver]) // 2
    margin = jnp.where((donor == ranking[0]) | (receiver == ranking[0]) | (lengths[receiver] == 0), 0, jnp.maximum(margin, 0))
    moved = jax.random.randint(jax.random.fold_in(own, 4), (amount // 2,), 0, 1 << 20) % (margin + 1)
    lengths = lengths.at[donor].add(-moved).at[receiver].add(moved)
    labels = jnp.searchsorted(jnp.cumsum(lengths), jnp.arange(rows * top), side="right").astype(jnp.int32)
    listing = labels.reshape(top, rows).T
    listing = listing[jax.random.permutation(jax.random.fold_in(own, 1), rows)]
    rotation = jax.random.randint(jax.random.fold_in(own, 2), (rows, 1), 0, top)
    return jnp.take_along_axis(listing, (jnp.arange(top)[None, :] + rotation) % top, axis=1)


def portions_of(number_of, total, bound, skew, full):
    loads = [(1 << 20) // math.isqrt(standing ** skew) + 1 for standing in range(1, number_of + 1)]
    largest = bound if full else min(bound, max(-(-total // number_of), total * loads[0] // sum(loads)))
    least = 1 if total - largest >= number_of - 1 else 0
    holding, surplus = [largest] + [least] * (number_of - 1), total - largest - least * (number_of - 1)
    while surplus > 0:
        movable = [i for i in range(1, number_of) if holding[i] < largest] or [i for i in range(1, number_of) if holding[i] < bound]
        whole, left = sum([loads[i] for i in movable]), surplus
        for i in movable:
            addition = min(bound - holding[i], max(1, left * loads[i] // whole), surplus)
            holding[i] = holding[i] + addition
            surplus = surplus - addition
    return np.array(holding)


def gaussian(key, extent, deviation, most, split=(), held_as=jnp.bfloat16):
    gain = steps_of(key, extent, split, -0.22, 0.18) if split else 1.0
    result = jax.random.normal(key, extent, jnp.float32) * deviation * gain
    return jnp.minimum(jnp.maximum(result, -most), most).astype(held_as)


def setup_inputs(seed: int = 0) -> dict:
    seeds = jax.random.split(jax.random.key(seed), 9)
    panels = draw_panels(jax.random.fold_in(seeds[8], 71), 0)
    tiles = gaussian(seeds[1], (NT, BN, 2 * BN), (2 * BN * TPD // NBD) ** -0.5, 0.109375, ((0, 32),))
    tile_dst = with_ends(jax.random.randint(seeds[2], (NT,), 0, NBD), jax.random.fold_in(seeds[2], 1), 0, NBD - 1).astype(jnp.int32)
    tile_src = with_ends(jax.random.randint(seeds[3], (NT,), 0, N_ROW * NBD), jax.random.fold_in(seeds[3], 1), 0, (N_ROW * NBD) - 1).astype(jnp.int32)
    geometry = gaussian(seeds[4], (NB, 6, BN), 1.0, 5.0, ((0, 32),), jnp.float32)
    areas = jnp.clip(jnp.exp(math.log(2.0) - 2.0794415 * jax.random.uniform(seeds[5], (NB, BN), jnp.float32) ** steps_of(seeds[5], (NB, BN), ((0, 32),), -0.2, 0.2)), 0.25, 2.0)
    block_owner_keys = jax.random.split(jax.random.fold_in(seeds[6], 1), NB // NBD)
    block_owner_turns = jax.random.permutation(jax.random.fold_in(seeds[6], 3), NB // NBD)
    block_owner = jax.vmap(lambda own, number: assign_block(jax.random.fold_in(seeds[6], 2), own, number, NBD, N_COL, 1, CAP, 2))(block_owner_keys, block_owner_turns).reshape((NB, 1))
    block_slot = with_ends(jax.random.randint(seeds[7], (NB,), 0, PD), jax.random.fold_in(seeds[7], 1), 0, PD - 1).astype(jnp.int32)
    return dict(panels=panels, tiles=tiles, tile_dst=tile_dst, tile_src=tile_src, geometry=geometry, areas=areas, block_owner=block_owner, block_slot=block_slot)


EPSILON = 1e-05

def make_basis(geometry, areas):
    normal = geometry[:, 0:3]
    place = geometry[:, 3:6]
    twist = jnp.stack([place[:, 1] * normal[:, 2] - place[:, 2] * normal[:, 1], place[:, 2] * normal[:, 0] - place[:, 0] * normal[:, 2], place[:, 0] * normal[:, 1] - place[:, 1] * normal[:, 0]], axis=1)
    weight = areas[:, None, :]
    return jnp.concatenate([weight * normal, weight * twist, weight, weight], axis=1)

def split_complex(images, freq_count, node_count):
    real_part = images[:, :freq_count, :node_count] - images[:, freq_count:, node_count:]
    imag_part = images[:, :freq_count, node_count:] + images[:, freq_count:, :node_count]
    return jnp.concatenate([real_part, imag_part], axis=1)

def energies(incident, field):
    freq_count = field.shape[1] // 2
    power = field[:, :freq_count] ** 2 + field[:, freq_count:] ** 2
    cross_power = incident[:, :freq_count] * field[:, :freq_count] + incident[:, freq_count:] * field[:, freq_count:]
    return (power, cross_power)

def block_moments(basis, power, cross_power):
    precise = lax.Precision.HIGHEST
    first_moments = jnp.einsum('bkn,bfn->bkf', basis[:, :7], power, precision=precise)
    last_moment = jnp.einsum('bn,bfn->bf', basis[:, 7], cross_power, precision=precise)
    joined = jnp.concatenate([first_moments, last_moment[:, None, :]], axis=1)
    return joined.reshape(joined.shape[0], -1)

def normalize(totals):
    return totals * lax.rsqrt(lax.optimization_barrier(jnp.mean(totals * totals, axis=1, keepdims=True)) + EPSILON)

def gradient_of(basis, power, cross_power, adjoint):
    precise = lax.Precision.HIGHEST
    freq_count = power.shape[1]
    shaped = adjoint.reshape(adjoint.shape[0], 8, freq_count)
    first_terms = jnp.einsum('bkf,bfn->bkn', shaped[:, :7], power, precision=precise)
    last_term = jnp.einsum('bf,bfn->bn', shaped[:, 7], cross_power, precision=precise)
    return (lax.optimization_barrier(jnp.sum(basis[:, :7] * first_terms, axis=1)) + basis[:, 7] * last_term) / freq_count

def reference(panels, tiles, tile_dst, tile_src, geometry, areas, block_owner, block_slot):
    precise = lax.Precision.HIGHEST
    block_total = panels.shape[0]
    rows_twice = panels.shape[1]
    freq_count = rows_twice // 2
    node_count = panels.shape[2]
    device_total = block_total // NBD
    tile_groups = tiles.reshape(device_total, TPD, node_count, 2 * node_count)
    dst_groups = tile_dst.reshape(device_total, TPD)
    src_groups = tile_src.reshape(device_total, TPD)

    def one_device(packed):
        device, device_tiles, device_dst, device_src = packed
        column = device % N_COL
        source = (device_src // NBD * N_COL + column) * NBD + device_src % NBD
        chosen = panels[source].astype(jnp.float32)
        images = jnp.einsum('tjn,tnm->tjm', chosen, device_tiles.astype(jnp.float32), precision=precise)
        terms = split_complex(images, freq_count, node_count)
        target = (device_dst[None, :] == jnp.arange(NBD, dtype=jnp.int32)[:, None]).astype(jnp.float32)
        return jnp.einsum('dt,tjn->djn', target, terms, precision=precise)
    near = lax.map(one_device, (jnp.arange(device_total, dtype=jnp.int32), tile_groups, dst_groups, src_groups))
    incident = panels.astype(jnp.float32)
    field = 0.5 * incident + near.reshape(block_total, rows_twice, node_count)
    power, cross_power = energies(incident, field)
    basis = make_basis(geometry, areas)
    moments = block_moments(basis, power, cross_power)
    block_index = jnp.arange(block_total, dtype=jnp.int32)
    row_index = block_index // NBD // N_COL
    particle = (row_index * N_COL + block_owner[:, 0]) * PD + block_slot
    totals = jax.ops.segment_sum(moments, particle, num_segments=PD * device_total)
    adjoint = normalize(totals)[particle]
    shape_gradient = gradient_of(basis, power, cross_power, adjoint)
    return (field, shape_gradient)
```

```python
import functools

import jax
import jax.numpy as jnp
from jax import lax
from jax.experimental import pallas as pl
from jax.experimental.pallas import tpu as pltpu
from jax.sharding import PartitionSpec as P

PD = 4
EPSILON = 1e-05
UNROLL = 4
COPIES = 8
MOMENTS = 8
F32 = jnp.float32
BF16 = jnp.bfloat16
VMEM_LIMIT = 28 << 20

VMEM_SPEC = pl.BlockSpec(memory_space=pltpu.VMEM)
SMEM_SPEC = pl.BlockSpec(memory_space=pltpu.SMEM)
ANY_SPEC = pl.BlockSpec(memory_space=pl.ANY)


def params():
    return pltpu.CompilerParams(vmem_limit_bytes=VMEM_LIMIT)


def parts_of(values, count):
    parts = []
    for _ in range(count - 1):
        part = values.astype(BF16)
        parts.append(part)
        values = values - part.astype(F32)
    parts.append(values.astype(BF16))
    return parts


def dot(left, right, transposed=False):
    axes = (((1,), (1 if transposed else 0,)), ((), ()))
    return lax.dot_general(left, right, axes, preferred_element_type=F32)


def dot_near_exact(left, right, transposed=False):
    left_high, left_low = parts_of(left, 2)
    right_high, right_low = parts_of(right, 2)
    return dot(left_high, right_high, transposed) + (
        dot(left_high, right_low, transposed) + dot(left_low, right_high, transposed)
    )


def block_mask(block_count, freq_count):
    shape = (block_count, block_count * freq_count)
    rows = lax.broadcasted_iota(jnp.int32, shape, 0)
    columns = lax.broadcasted_iota(jnp.int32, shape, 1)
    return (columns // freq_count == rows).astype(F32)


def fill_panels(sources, held):
    depth = sources[0].shape[0]
    for index, source in enumerate(sources):
        held[index * depth : (index + 1) * depth] = source[...]
    held[len(sources) * depth] = jnp.zeros(held.shape[1:], held.dtype)


def add_stage(stage, width, plan, held, tiles, total):
    def body(step, carry):
        base = step * UNROLL
        images = [
            dot(held[plan[width + base + lane]], tiles[plan[base + lane]])
            for lane in range(UNROLL)
        ]
        for lane in range(UNROLL):
            target = plan[2 * width + base + lane]
            total[target] += images[lane]
        return carry

    lax.fori_loop(plan[3 * width + stage], plan[3 * width + stage + 1], body, 0)


def first_kernel(bounds, width, src, dst, panels, tiles, held_tiles, total, plan, held, sems):
    tile_count = tiles.shape[0]
    depth = panels.shape[0]
    per_copy = tile_count // COPIES
    copies = [
        pltpu.make_async_copy(
            tiles.at[pl.ds(i * per_copy, per_copy)],
            held_tiles.at[pl.ds(i * per_copy, per_copy)],
            sems.at[i],
        )
        for i in range(COPIES)
    ]
    for copy in copies:
        copy.start()
    me = lax.axis_index("row")
    position = jnp.int32(0)
    for stage in range(len(bounds) - 1):
        low, high = bounds[stage], bounds[stage + 1]
        plan[3 * width + stage] = position // UNROLL

        def place(t, position, low=low, high=high):
            source = src[t]
            hop = (source // depth) ^ me
            plan[position] = t
            plan[width + position] = (hop - low) * depth + source % depth
            plan[2 * width + position] = dst[t]
            return position + ((hop >= low) & (hop < high)).astype(jnp.int32)

        position = lax.fori_loop(0, tile_count, place, position)
        for lane in range(UNROLL):
            plan[position + lane] = 0
            plan[width + position + lane] = (high - low) * depth
            plan[2 * width + position + lane] = 0
        position = (position + UNROLL - 1) // UNROLL * UNROLL
    plan[3 * width + len(bounds) - 1] = position // UNROLL
    total[...] = jnp.zeros_like(total)
    fill_panels([panels], held)
    for copy in copies:
        copy.wait()
    add_stage(0, width, plan, held, held_tiles, total)


def middle_kernel(width, count, plan, owner, slot, *refs):
    sources = refs[:count]
    tiles, start, place, areas, total, basis, spread, held = refs[count:]
    block_count = areas.shape[0]
    fill_panels(sources, held)
    total[...] = start[...]
    nx, ny, nz, px, py, pz = [place[i] for i in range(6)]
    weight = areas[...]
    rows = [nx, ny, nz, py * nz - pz * ny, pz * nx - px * nz, px * ny - py * nx]
    for index, row in enumerate(rows):
        basis[index * block_count : (index + 1) * block_count] = weight * row
    for index in range(len(rows), MOMENTS):
        basis[index * block_count : (index + 1) * block_count] = weight
    freq_count = spread.shape[0] // block_count
    shape = (freq_count, spread.shape[1])
    lanes = lax.broadcasted_iota(jnp.int32, shape, 1)
    same = lanes % freq_count == lax.broadcasted_iota(jnp.int32, shape, 0)
    for block in range(block_count):
        particle = owner[block] * PD + slot[block]
        chosen = same & (lanes // freq_count == particle)
        spread[block * freq_count : (block + 1) * freq_count] = jnp.where(
            chosen, 1.0, 0.0
        ).astype(BF16)
    add_stage(1, width, plan, held, tiles, total)


def field_kernel(width, count, plan, *refs):
    sources = refs[:count]
    panels, tiles, start, basis, spread = refs[count : count + 5]
    field, table, powers, crosses, held, total = refs[count + 5 :]
    block_count, rows_twice, node_count = panels.shape
    freq_count = rows_twice // 2
    fill_panels(sources, held)
    total[...] = start[...]
    add_stage(2, width, plan, held, tiles, total)
    for block in range(block_count):
        image = total[block]
        incident = panels[block].astype(F32)
        real_in, imag_in = incident[:freq_count], incident[freq_count:]
        real = 0.5 * real_in + (
            image[:freq_count, :node_count] - image[freq_count:, node_count:]
        )
        imag = 0.5 * imag_in + (
            image[:freq_count, node_count:] + image[freq_count:, :node_count]
        )
        field[block, :freq_count] = real
        field[block, freq_count:] = imag
        span = slice(block * freq_count, (block + 1) * freq_count)
        powers[span] = real * real + imag * imag
        crosses[span] = real_in * real + imag_in * imag
    last = (MOMENTS - 1) * block_count
    first_moments = dot_near_exact(basis[:last], powers[...], True)
    last_moment = dot_near_exact(basis[last:], crosses[...], True)
    mask = block_mask(block_count, freq_count)
    pieces = [
        jnp.sum(mask * first_moments[k * block_count : (k + 1) * block_count], axis=0, keepdims=True)
        for k in range(MOMENTS - 1)
    ]
    pieces.append(jnp.sum(mask * last_moment, axis=0, keepdims=True))
    moments = jnp.concatenate(pieces, axis=0)
    joined = dot(jnp.concatenate(parts_of(moments, 3), axis=0), spread[...])
    table[...] = joined[:MOMENTS] + (joined[MOMENTS : 2 * MOMENTS] + joined[2 * MOMENTS :])


def gradient_kernel(count, *refs):
    tables = refs[:count]
    basis, spread, powers, crosses, gradient = refs[count:]
    block_count = gradient.shape[0]
    freq_count = powers.shape[0] // block_count
    summed = tables[0][...]
    for table in tables[1:]:
        summed = summed + table[...]
    joined = dot(jnp.concatenate(parts_of(summed, 3), axis=0), spread[...], True)
    totals = joined[:MOMENTS] + (joined[MOMENTS : 2 * MOMENTS] + joined[2 * MOMENTS :])
    mask = block_mask(block_count, freq_count)
    squares = jnp.sum(totals * totals, axis=0, keepdims=True)
    mean = jnp.sum(mask * squares, axis=1, keepdims=True) / (MOMENTS * freq_count)
    scale = lax.rsqrt(mean + EPSILON) / freq_count
    spots = [mask * totals[k : k + 1] for k in range(MOMENTS)]
    first_terms = dot_near_exact(jnp.concatenate(spots[:-1], axis=0), powers[...])
    last_term = dot_near_exact(spots[-1], crosses[...])
    result = basis[(MOMENTS - 1) * block_count :] * last_term
    for k in range(MOMENTS - 1):
        span = slice(k * block_count, (k + 1) * block_count)
        result = result + basis[span] * first_terms[span]
    gradient[...] = result * scale


def exchange(values, axis, hop):
    pairs = [(i, i ^ hop) for i in range(lax.axis_size(axis))]
    return lax.ppermute(values, axis, pairs)


def shards(panels, tiles, tile_dst, tile_src, geometry, areas, block_owner, block_slot):
    block_count, rows_twice, node_count = panels.shape
    freq_count = rows_twice // 2
    tile_count = tiles.shape[0]
    row_count = lax.axis_size("row")
    group_count = lax.axis_size("col")
    particle_count = group_count * PD
    bounds = (0, 1, row_count - 2, row_count)
    width = -(-(tile_count + 4 * UNROLL) // 128) * 128
    image_shape = (block_count, rows_twice, 2 * node_count)

    def held(count):
        return pltpu.VMEM((count * block_count + 1, rows_twice, node_count), BF16)

    hops = {0: panels}
    for hop in [row_count - 2, *range(row_count - 4, 0, -2)]:
        hops[hop] = exchange(panels, "row", hop)
    hops[1] = exchange(panels, "row", 1)
    for hop in range(2, row_count, 2):
        hops[hop + 1] = exchange(hops[hop], "row", 1)

    held_tiles, early, plan = pl.pallas_call(
        functools.partial(first_kernel, bounds, width),
        out_shape=(
            pltpu.VMEM(tiles.shape, tiles.dtype),
            pltpu.VMEM(image_shape, F32),
            jax.ShapeDtypeStruct((3 * width + 128,), jnp.int32),
        ),
        in_specs=[SMEM_SPEC, SMEM_SPEC, VMEM_SPEC, ANY_SPEC],
        out_specs=(VMEM_SPEC, VMEM_SPEC, SMEM_SPEC),
        scratch_shapes=[held(1), pltpu.SemaphoreType.DMA((COPIES,))],
        compiler_params=params(),
        cost_estimate=pl.CostEstimate(
            flops=0, bytes_accessed=2 * tiles.size * 2, transcendentals=0
        ),
        name="first_stage",
    )(tile_src, tile_dst, panels, tiles)

    middle = [hops[j] for j in range(bounds[1], bounds[2])]
    basis_shape = (MOMENTS * block_count, node_count)
    spread_shape = (block_count * freq_count, particle_count * freq_count)
    power_shape = (block_count * freq_count, node_count)
    table_shape = (MOMENTS, particle_count * freq_count)
    partial_field, basis, spread = pl.pallas_call(
        functools.partial(middle_kernel, width, len(middle)),
        out_shape=(
            pltpu.VMEM(image_shape, F32),
            pltpu.VMEM(basis_shape, F32),
            pltpu.VMEM(spread_shape, BF16),
        ),
        in_specs=[SMEM_SPEC] * 3 + [VMEM_SPEC] * (len(middle) + 4),
        out_specs=(VMEM_SPEC,) * 3,
        scratch_shapes=[held(len(middle))],
        compiler_params=params(),
        name="middle_stage",
    )(
        plan,
        block_owner[:, 0],
        block_slot,
        *middle,
        held_tiles,
        early,
        jnp.transpose(geometry, (1, 0, 2)),
        areas,
    )

    late = [hops[j] for j in range(bounds[2], bounds[3])]
    field, table, powers, crosses = pl.pallas_call(
        functools.partial(field_kernel, width, len(late)),
        out_shape=(
            jax.ShapeDtypeStruct(panels.shape, F32),
            pltpu.VMEM(table_shape, F32),
            pltpu.VMEM(power_shape, F32),
            pltpu.VMEM(power_shape, F32),
        ),
        in_specs=[SMEM_SPEC] + [VMEM_SPEC] * (len(late) + 5),
        out_specs=(VMEM_SPEC,) * 4,
        scratch_shapes=[held(len(late)), pltpu.VMEM(image_shape, F32)],
        compiler_params=params(),
        name="field_stage",
    )(plan, *late, panels, held_tiles, partial_field, basis, spread)

    tables = [table]
    for hop in range(1, group_count):
        tables.append(exchange(table, "col", hop))

    gradient = pl.pallas_call(
        functools.partial(gradient_kernel, len(tables)),
        out_shape=jax.ShapeDtypeStruct((block_count, node_count), F32),
        in_specs=[VMEM_SPEC] * (len(tables) + 4),
        out_specs=VMEM_SPEC,
        compiler_params=params(),
        name="gradient_stage",
    )(*tables, basis, spread, powers, crosses)
    return (field, gradient)


def solution(mesh):
    in_specs = (
        P(("row", "col"), None, None),
        P(("row", "col"), None, None),
        P(("row", "col")),
        P(("row", "col")),
        P(("row", "col"), None, None),
        P(("row", "col"), None),
        P(("row", "col"), None),
        P(("row", "col")),
    )
    out_specs = (P(("row", "col"), None, None), P(("row", "col"), None))
    return jax.shard_map(shards, mesh=mesh, in_specs=in_specs, out_specs=out_specs, check_vma=False)
```

```python
import functools

import jax
import jax.numpy as jnp
from jax import lax
from jax.experimental import pallas as pl
from jax.experimental.pallas import tpu as pltpu
from jax.sharding import PartitionSpec as P

PD = 4
EPSILON = 1e-05
UNROLL = 4
COPIES = 8
MOMENTS = 8
F32 = jnp.float32
BF16 = jnp.bfloat16
VMEM_LIMIT = 8 << 20
FIRST_LIMIT = 44 << 20

VMEM_SPEC = pl.BlockSpec(memory_space=pltpu.VMEM)
SMEM_SPEC = pl.BlockSpec(memory_space=pltpu.SMEM)
HBM_SPEC = pl.BlockSpec(memory_space=pltpu.HBM)


def params(limit=VMEM_LIMIT):
    return pltpu.CompilerParams(vmem_limit_bytes=limit)


def parts_of(values, count):
    parts = []
    for _ in range(count - 1):
        part = values.astype(BF16)
        parts.append(part)
        values = values - part.astype(F32)
    parts.append(values.astype(BF16))
    return parts


def dot(left, right, transposed=False):
    axes = (((1,), (1 if transposed else 0,)), ((), ()))
    return lax.dot_general(left, right, axes, preferred_element_type=F32)


def dot_near_exact(left, right, transposed=False):
    left_high, left_low = parts_of(left, 2)
    right_high, right_low = parts_of(right, 2)
    return dot(left_high, right_high, transposed) + (
        dot(left_high, right_low, transposed) + dot(left_low, right_high, transposed)
    )


def block_mask(block_count, freq_count):
    shape = (block_count, block_count * freq_count)
    rows = lax.broadcasted_iota(jnp.int32, shape, 0)
    columns = lax.broadcasted_iota(jnp.int32, shape, 1)
    return (columns // freq_count == rows).astype(F32)


def fill_panels(sources, held):
    depth = sources[0].shape[0]
    for index, source in enumerate(sources):
        held[index * depth : (index + 1) * depth] = source[...]
    held[len(sources) * depth] = jnp.zeros(held.shape[1:], held.dtype)


def add_stage(stage, width, plan, held, tiles, total):
    def body(step, carry):
        base = step * UNROLL
        images = [
            dot(held[plan[width + base + lane]], tiles[plan[base + lane]])
            for lane in range(UNROLL)
        ]
        for lane in range(UNROLL):
            target = plan[2 * width + base + lane]
            total[target] += images[lane]
        return carry

    lax.fori_loop(plan[3 * width + stage], plan[3 * width + stage + 1], body, 0)


def first_kernel(bounds, width, src, dst, panels, tiles, held_tiles, total, plan, held, sems):
    tile_count = tiles.shape[0]
    depth = panels.shape[0]
    per_copy = tile_count // COPIES
    copies = [
        pltpu.make_async_copy(
            tiles.at[pl.ds(i * per_copy, per_copy)],
            held_tiles.at[pl.ds(i * per_copy, per_copy)],
            sems.at[i],
        )
        for i in range(COPIES)
    ]
    for copy in copies:
        copy.start()
    me = lax.axis_index("row")
    position = jnp.int32(0)
    for stage in range(len(bounds) - 1):
        low, high = bounds[stage], bounds[stage + 1]
        plan[3 * width + stage] = position // UNROLL

        def place(t, position, low=low, high=high):
            source = src[t]
            hop = (source // depth) ^ me
            plan[position] = t
            plan[width + position] = (hop - low) * depth + source % depth
            plan[2 * width + position] = dst[t]
            return position + ((hop >= low) & (hop < high)).astype(jnp.int32)

        position = lax.fori_loop(0, tile_count, place, position)
        for lane in range(UNROLL):
            plan[position + lane] = 0
            plan[width + position + lane] = (high - low) * depth
            plan[2 * width + position + lane] = 0
        position = (position + UNROLL - 1) // UNROLL * UNROLL
    plan[3 * width + len(bounds) - 1] = position // UNROLL
    total[...] = jnp.zeros_like(total)
    fill_panels([panels], held)
    for copy in copies:
        copy.wait()
    add_stage(0, width, plan, held, held_tiles, total)


def middle_kernel(width, count, plan, owner, slot, *refs):
    sources = refs[:count]
    tiles, start, place, areas, total, basis, spread, held = refs[count:]
    block_count = areas.shape[0]
    fill_panels(sources, held)
    total[...] = start[...]
    nx, ny, nz, px, py, pz = [place[i] for i in range(6)]
    weight = areas[...]
    rows = [nx, ny, nz, py * nz - pz * ny, pz * nx - px * nz, px * ny - py * nx]
    for index, row in enumerate(rows):
        basis[index * block_count : (index + 1) * block_count] = weight * row
    for index in range(len(rows), MOMENTS):
        basis[index * block_count : (index + 1) * block_count] = weight
    freq_count = spread.shape[0] // block_count
    shape = (freq_count, spread.shape[1])
    lanes = lax.broadcasted_iota(jnp.int32, shape, 1)
    same = lanes % freq_count == lax.broadcasted_iota(jnp.int32, shape, 0)
    for block in range(block_count):
        particle = owner[block] * PD + slot[block]
        chosen = same & (lanes // freq_count == particle)
        spread[block * freq_count : (block + 1) * freq_count] = jnp.where(
            chosen, 1.0, 0.0
        ).astype(BF16)
    add_stage(1, width, plan, held, tiles, total)


def field_kernel(width, count, plan, *refs):
    sources = refs[:count]
    panels, tiles, start, basis, spread = refs[count : count + 5]
    field, table, powers, crosses, held, total = refs[count + 5 :]
    block_count, rows_twice, node_count = panels.shape
    freq_count = rows_twice // 2
    fill_panels(sources, held)
    total[...] = start[...]
    add_stage(2, width, plan, held, tiles, total)
    for block in range(block_count):
        image = total[block]
        incident = panels[block].astype(F32)
        real_in, imag_in = incident[:freq_count], incident[freq_count:]
        real = 0.5 * real_in + (
            image[:freq_count, :node_count] - image[freq_count:, node_count:]
        )
        imag = 0.5 * imag_in + (
            image[:freq_count, node_count:] + image[freq_count:, :node_count]
        )
        field[block, :freq_count] = real
        field[block, freq_count:] = imag
        span = slice(block * freq_count, (block + 1) * freq_count)
        powers[span] = real * real + imag * imag
        crosses[span] = real_in * real + imag_in * imag
    last = (MOMENTS - 1) * block_count
    first_moments = dot_near_exact(basis[:last], powers[...], True)
    last_moment = dot_near_exact(basis[last:], crosses[...], True)
    mask = block_mask(block_count, freq_count)
    pieces = [
        jnp.sum(mask * first_moments[k * block_count : (k + 1) * block_count], axis=0, keepdims=True)
        for k in range(MOMENTS - 1)
    ]
    pieces.append(jnp.sum(mask * last_moment, axis=0, keepdims=True))
    moments = jnp.concatenate(pieces, axis=0)
    joined = dot(jnp.concatenate(parts_of(moments, 3), axis=0), spread[...])
    table[...] = joined[:MOMENTS] + (joined[MOMENTS : 2 * MOMENTS] + joined[2 * MOMENTS :])


def gradient_kernel(count, *refs):
    tables = refs[:count]
    basis, spread, powers, crosses, gradient = refs[count:]
    block_count = gradient.shape[0]
    freq_count = powers.shape[0] // block_count
    summed = tables[0][...]
    for table in tables[1:]:
        summed = summed + table[...]
    joined = dot(jnp.concatenate(parts_of(summed, 3), axis=0), spread[...], True)
    totals = joined[:MOMENTS] + (joined[MOMENTS : 2 * MOMENTS] + joined[2 * MOMENTS :])
    mask = block_mask(block_count, freq_count)
    squares = jnp.sum(totals * totals, axis=0, keepdims=True)
    mean = jnp.sum(mask * squares, axis=1, keepdims=True) / (MOMENTS * freq_count)
    scale = lax.rsqrt(mean + EPSILON) / freq_count
    spots = [mask * totals[k : k + 1] for k in range(MOMENTS)]
    first_terms = dot_near_exact(jnp.concatenate(spots[:-1], axis=0), powers[...])
    last_term = dot_near_exact(spots[-1], crosses[...])
    result = basis[(MOMENTS - 1) * block_count :] * last_term
    for k in range(MOMENTS - 1):
        span = slice(k * block_count, (k + 1) * block_count)
        result = result + basis[span] * first_terms[span]
    gradient[...] = result * scale


def exchange(values, axis, hop):
    pairs = [(i, i ^ hop) for i in range(lax.axis_size(axis))]
    return lax.ppermute(values, axis, pairs)


def shards(panels, tiles, tile_dst, tile_src, geometry, areas, block_owner, block_slot):
    block_count, rows_twice, node_count = panels.shape
    freq_count = rows_twice // 2
    tile_count = tiles.shape[0]
    row_count = lax.axis_size("row")
    group_count = lax.axis_size("col")
    particle_count = group_count * PD
    bounds = (0, 1, row_count - 2, row_count)
    width = -(-(tile_count + 4 * UNROLL) // 128) * 128
    image_shape = (block_count, rows_twice, 2 * node_count)

    def held(count):
        return pltpu.VMEM((count * block_count + 1, rows_twice, node_count), BF16)

    hops = {0: panels}
    for hop in [row_count - 2, *range(row_count - 4, 0, -2)]:
        hops[hop] = exchange(panels, "row", hop)
    hops[1] = exchange(panels, "row", 1)
    held_tiles, early, plan = pl.pallas_call(
        functools.partial(first_kernel, bounds, width),
        out_shape=(
            pltpu.VMEM(tiles.shape, tiles.dtype),
            pltpu.VMEM(image_shape, F32),
            jax.ShapeDtypeStruct((3 * width + 128,), jnp.int32),
        ),
        in_specs=[SMEM_SPEC, SMEM_SPEC, VMEM_SPEC, HBM_SPEC],
        out_specs=(VMEM_SPEC, VMEM_SPEC, SMEM_SPEC),
        scratch_shapes=[held(1), pltpu.SemaphoreType.DMA((COPIES,))],
        compiler_params=params(FIRST_LIMIT),
        cost_estimate=pl.CostEstimate(
            flops=0, bytes_accessed=2 * tiles.size * 2, transcendentals=0
        ),
        name="first_stage",
    )(tile_src, tile_dst, panels, tiles)

    for hop in range(2, row_count, 2):
        hops[hop], plan = lax.optimization_barrier((hops[hop], plan))
        hops[hop + 1] = exchange(hops[hop], "row", 1)

    middle = [hops[j] for j in range(bounds[1], bounds[2])]
    basis_shape = (MOMENTS * block_count, node_count)
    spread_shape = (block_count * freq_count, particle_count * freq_count)
    power_shape = (block_count * freq_count, node_count)
    table_shape = (MOMENTS, particle_count * freq_count)
    partial_field, basis, spread = pl.pallas_call(
        functools.partial(middle_kernel, width, len(middle)),
        out_shape=(
            pltpu.VMEM(image_shape, F32),
            pltpu.VMEM(basis_shape, F32),
            pltpu.VMEM(spread_shape, BF16),
        ),
        in_specs=[SMEM_SPEC] * 3 + [VMEM_SPEC] * (len(middle) + 4),
        out_specs=(VMEM_SPEC,) * 3,
        scratch_shapes=[held(len(middle))],
        compiler_params=params(),
        name="middle_stage",
    )(
        plan,
        block_owner[:, 0],
        block_slot,
        *middle,
        held_tiles,
        early,
        jnp.transpose(geometry, (1, 0, 2)),
        areas,
    )

    late = [hops[j] for j in range(bounds[2], bounds[3])]
    field, table, powers, crosses = pl.pallas_call(
        functools.partial(field_kernel, width, len(late)),
        out_shape=(
            jax.ShapeDtypeStruct(panels.shape, F32),
            pltpu.VMEM(table_shape, F32),
            pltpu.VMEM(power_shape, F32),
            pltpu.VMEM(power_shape, F32),
        ),
        in_specs=[SMEM_SPEC] + [VMEM_SPEC] * (len(late) + 5),
        out_specs=(VMEM_SPEC,) * 4,
        scratch_shapes=[held(len(late)), pltpu.VMEM(image_shape, F32)],
        compiler_params=params(),
        name="field_stage",
    )(plan, *late, panels, held_tiles, partial_field, basis, spread)

    tables = [table]
    for hop in range(1, group_count):
        tables.append(exchange(table, "col", hop))

    gradient = pl.pallas_call(
        functools.partial(gradient_kernel, len(tables)),
        out_shape=jax.ShapeDtypeStruct((block_count, node_count), F32),
        in_specs=[VMEM_SPEC] * (len(tables) + 4),
        out_specs=VMEM_SPEC,
        compiler_params=params(),
        name="gradient_stage",
    )(*tables, basis, spread, powers, crosses)
    return (field, gradient)


def solution(mesh):
    in_specs = (
        P(("row", "col"), None, None),
        P(("row", "col"), None, None),
        P(("row", "col")),
        P(("row", "col")),
        P(("row", "col"), None, None),
        P(("row", "col"), None),
        P(("row", "col"), None),
        P(("row", "col")),
    )
    out_specs = (P(("row", "col"), None, None), P(("row", "col"), None))
    return jax.shard_map(shards, mesh=mesh, in_specs=in_specs, out_specs=out_specs, check_vma=False)
```

```python
import functools

import jax
import jax.numpy as jnp
from jax import lax
from jax.experimental import pallas as pl
from jax.experimental.pallas import tpu as pltpu
from jax.sharding import PartitionSpec as P

PD = 4
EPSILON = 1e-05
UNROLL = 4
COPIES = 8
MOMENTS = 8
F32 = jnp.float32
BF16 = jnp.bfloat16
VMEM_LIMIT = 8 << 20
FIRST_LIMIT = 44 << 20

VMEM_SPEC = pl.BlockSpec(memory_space=pltpu.VMEM)
SMEM_SPEC = pl.BlockSpec(memory_space=pltpu.SMEM)
HBM_SPEC = pl.BlockSpec(memory_space=pltpu.HBM)


def params(limit=VMEM_LIMIT):
    return pltpu.CompilerParams(vmem_limit_bytes=limit)


def parts_of(values, count):
    parts = []
    for _ in range(count - 1):
        part = values.astype(BF16)
        parts.append(part)
        values = values - part.astype(F32)
    parts.append(values.astype(BF16))
    return parts


def dot(left, right, transposed=False):
    axes = (((1,), (1 if transposed else 0,)), ((), ()))
    return lax.dot_general(left, right, axes, preferred_element_type=F32)


def dot_near_exact(left, right, transposed=False):
    left_high, left_low = parts_of(left, 2)
    right_high, right_low = parts_of(right, 2)
    return dot(left_high, right_high, transposed) + (
        dot(left_high, right_low, transposed) + dot(left_low, right_high, transposed)
    )


def block_mask(block_count, freq_count):
    shape = (block_count, block_count * freq_count)
    rows = lax.broadcasted_iota(jnp.int32, shape, 0)
    columns = lax.broadcasted_iota(jnp.int32, shape, 1)
    return (columns // freq_count == rows).astype(F32)


def fill_panels(sources, held):
    depth = sources[0].shape[0]
    for index, source in enumerate(sources):
        held[index * depth : (index + 1) * depth] = source[...]
    held[len(sources) * depth] = jnp.zeros(held.shape[1:], held.dtype)


def add_stage(stage, width, plan, held, tiles, total):
    def body(step, carry):
        base = step * UNROLL
        images = [
            dot(held[plan[width + base + lane]], tiles[plan[base + lane]])
            for lane in range(UNROLL)
        ]
        for lane in range(UNROLL):
            target = plan[2 * width + base + lane]
            total[target] += images[lane]
        return carry

    lax.fori_loop(plan[3 * width + stage], plan[3 * width + stage + 1], body, 0)


def load_kernel(
    bounds, width, freq_count, src, dst, owner, slot, place, areas, tiles,
    held_tiles, basis, spread, plan, sems,
):
    tile_count = tiles.shape[0]
    block_count = areas.shape[0]
    per_copy = tile_count // COPIES
    copies = [
        pltpu.make_async_copy(
            tiles.at[pl.ds(i * per_copy, per_copy)],
            held_tiles.at[pl.ds(i * per_copy, per_copy)],
            sems.at[i],
        )
        for i in range(COPIES)
    ]
    for copy in copies:
        copy.start()
    me = lax.axis_index("row")
    position = jnp.int32(0)
    for stage, hops in enumerate(bounds):
        plan[3 * width + stage] = position // UNROLL
        position = lax.fori_loop(
            0, tile_count, functools.partial(place_tile, width, hops, block_count, me, src, dst, plan), position
        )
        for lane in range(UNROLL):
            plan[position + lane] = 0
            plan[width + position + lane] = len(hops) * block_count
            plan[2 * width + position + lane] = 0
        position = (position + UNROLL - 1) // UNROLL * UNROLL
    plan[3 * width + len(bounds)] = position // UNROLL
    nx, ny, nz, px, py, pz = [place[i] for i in range(6)]
    weight = areas[...]
    rows = [nx, ny, nz, py * nz - pz * ny, pz * nx - px * nz, px * ny - py * nx]
    for index, row in enumerate(rows):
        basis[index * block_count : (index + 1) * block_count] = weight * row
    for index in range(len(rows), MOMENTS):
        basis[index * block_count : (index + 1) * block_count] = weight
    shape = (freq_count, spread.shape[1])
    lanes = lax.broadcasted_iota(jnp.int32, shape, 1)
    same = lanes % freq_count == lax.broadcasted_iota(jnp.int32, shape, 0)
    for block in range(block_count):
        particle = owner[block] * PD + slot[block]
        chosen = same & (lanes // freq_count == particle)
        spread[block * freq_count : (block + 1) * freq_count] = jnp.where(
            chosen, 1.0, 0.0
        ).astype(BF16)
    for copy in copies:
        copy.wait()


def place_tile(width, hops, depth, me, src, dst, plan, t, position):
    source = src[t]
    hop = (source // depth) ^ me
    here = hop == hops[0]
    row = jnp.int32(0)
    for index, other in enumerate(hops[1:], 1):
        here = here | (hop == other)
        row = jnp.where(hop == other, index, row)
    plan[position] = t
    plan[width + position] = row * depth + source % depth
    plan[2 * width + position] = dst[t]
    return position + here.astype(jnp.int32)


def near_kernel(stage, width, count, begin, plan, *refs):
    sources, refs = refs[:count], refs[count:]
    tiles, refs = refs[0], refs[1:]
    if begin:
        total, held = refs
        total[...] = jnp.zeros_like(total)
    else:
        start, total, held = refs
        total[...] = start[...]
    fill_panels(sources, held)
    add_stage(stage, width, plan, held, tiles, total)


def field_kernel(stage, width, count, plan, *refs):
    sources = refs[:count]
    panels, tiles, start, basis, spread = refs[count : count + 5]
    field, table, powers, crosses, held, total = refs[count + 5 :]
    block_count, rows_twice, node_count = panels.shape
    freq_count = rows_twice // 2
    fill_panels(sources, held)
    total[...] = start[...]
    add_stage(stage, width, plan, held, tiles, total)
    for block in range(block_count):
        image = total[block]
        incident = panels[block].astype(F32)
        real_in, imag_in = incident[:freq_count], incident[freq_count:]
        real = 0.5 * real_in + (
            image[:freq_count, :node_count] - image[freq_count:, node_count:]
        )
        imag = 0.5 * imag_in + (
            image[:freq_count, node_count:] + image[freq_count:, :node_count]
        )
        field[block, :freq_count] = real
        field[block, freq_count:] = imag
        span = slice(block * freq_count, (block + 1) * freq_count)
        powers[span] = real * real + imag * imag
        crosses[span] = real_in * real + imag_in * imag
    last = (MOMENTS - 1) * block_count
    first_moments = dot_near_exact(basis[:last], powers[...], True)
    last_moment = dot_near_exact(basis[last:], crosses[...], True)
    mask = block_mask(block_count, freq_count)
    pieces = [
        jnp.sum(mask * first_moments[k * block_count : (k + 1) * block_count], axis=0, keepdims=True)
        for k in range(MOMENTS - 1)
    ]
    pieces.append(jnp.sum(mask * last_moment, axis=0, keepdims=True))
    moments = jnp.concatenate(pieces, axis=0)
    joined = dot(jnp.concatenate(parts_of(moments, 3), axis=0), spread[...])
    table[...] = joined[:MOMENTS] + (joined[MOMENTS : 2 * MOMENTS] + joined[2 * MOMENTS :])


def gradient_kernel(count, *refs):
    tables = refs[:count]
    basis, spread, powers, crosses, gradient = refs[count:]
    block_count = gradient.shape[0]
    freq_count = powers.shape[0] // block_count
    summed = tables[0][...]
    for table in tables[1:]:
        summed = summed + table[...]
    joined = dot(jnp.concatenate(parts_of(summed, 3), axis=0), spread[...], True)
    totals = joined[:MOMENTS] + (joined[MOMENTS : 2 * MOMENTS] + joined[2 * MOMENTS :])
    mask = block_mask(block_count, freq_count)
    squares = jnp.sum(totals * totals, axis=0, keepdims=True)
    mean = jnp.sum(mask * squares, axis=1, keepdims=True) / (MOMENTS * freq_count)
    scale = lax.rsqrt(mean + EPSILON) / freq_count
    spots = [mask * totals[k : k + 1] for k in range(MOMENTS)]
    first_terms = dot_near_exact(jnp.concatenate(spots[:-1], axis=0), powers[...])
    last_term = dot_near_exact(spots[-1], crosses[...])
    result = basis[(MOMENTS - 1) * block_count :] * last_term
    for k in range(MOMENTS - 1):
        span = slice(k * block_count, (k + 1) * block_count)
        result = result + basis[span] * first_terms[span]
    gradient[...] = result * scale


def exchange(values, axis, hop):
    pairs = [(i, i ^ hop) for i in range(lax.axis_size(axis))]
    return lax.ppermute(values, axis, pairs)


def shards(panels, tiles, tile_dst, tile_src, geometry, areas, block_owner, block_slot):
    block_count, rows_twice, node_count = panels.shape
    freq_count = rows_twice // 2
    tile_count = tiles.shape[0]
    row_count = lax.axis_size("row")
    group_count = lax.axis_size("col")
    particle_count = group_count * PD
    direct = list(range(2, row_count, 2))
    soon, late = direct[:-1], direct[-1]
    stages = ([0, 1], soon, [hop + 1 for hop in soon] + [late], [late + 1])
    width = -(-(tile_count + (len(stages) + 1) * UNROLL) // 128) * 128
    image_shape = (block_count, rows_twice, 2 * node_count)
    basis_shape = (MOMENTS * block_count, node_count)
    spread_shape = (block_count * freq_count, particle_count * freq_count)
    power_shape = (block_count * freq_count, node_count)
    table_shape = (MOMENTS, particle_count * freq_count)

    def held(stage):
        return pltpu.VMEM((len(stages[stage]) * block_count + 1, rows_twice, node_count), BF16)

    hops = {0: panels}
    for hop in direct:
        hops[hop] = exchange(panels, "row", hop)
    hops[1] = exchange(panels, "row", 1)

    held_tiles, basis, spread, plan = pl.pallas_call(
        functools.partial(load_kernel, stages, width, freq_count),
        out_shape=(
            pltpu.VMEM(tiles.shape, tiles.dtype),
            pltpu.VMEM(basis_shape, F32),
            pltpu.VMEM(spread_shape, BF16),
            pltpu.SMEM((3 * width + 128,), jnp.int32),
        ),
        in_specs=[SMEM_SPEC] * 4 + [VMEM_SPEC] * 2 + [HBM_SPEC],
        out_specs=(VMEM_SPEC,) * 3 + (SMEM_SPEC,),
        scratch_shapes=[pltpu.SemaphoreType.DMA((COPIES,))],
        compiler_params=params(FIRST_LIMIT),
        cost_estimate=pl.CostEstimate(
            flops=0, bytes_accessed=2 * tiles.size * 2, transcendentals=0
        ),
        name="load_stage",
    )(tile_src, tile_dst, block_owner[:, 0], block_slot, jnp.transpose(geometry, (1, 0, 2)), areas, tiles)

    def near(stage, total):
        begin = total is None
        sources = [hops[hop] for hop in stages[stage]]
        return pl.pallas_call(
            functools.partial(near_kernel, stage, width, len(sources), begin),
            out_shape=pltpu.VMEM(image_shape, F32),
            in_specs=[SMEM_SPEC] + [VMEM_SPEC] * (len(sources) + (1 if begin else 2)),
            out_specs=VMEM_SPEC,
            scratch_shapes=[held(stage)],
            compiler_params=params(),
            name="near_stage",
        )(plan, *sources, held_tiles, *([] if begin else [total]))

    total = near(0, None)
    for hop in soon:
        hops[hop], total = lax.optimization_barrier((hops[hop], total))
        hops[hop + 1] = exchange(hops[hop], "row", 1)
    total = near(1, total)
    hops[late], total = lax.optimization_barrier((hops[late], total))
    hops[late + 1] = exchange(hops[late], "row", 1)
    total = near(2, total)

    field, table, powers, crosses = pl.pallas_call(
        functools.partial(field_kernel, 3, width, 1),
        out_shape=(
            pltpu.VMEM(panels.shape, F32),
            pltpu.VMEM(table_shape, F32),
            pltpu.VMEM(power_shape, F32),
            pltpu.VMEM(power_shape, F32),
        ),
        in_specs=[SMEM_SPEC] + [VMEM_SPEC] * 6,
        out_specs=(VMEM_SPEC,) * 4,
        scratch_shapes=[held(3), pltpu.VMEM(image_shape, F32)],
        compiler_params=params(),
        name="field_stage",
    )(plan, hops[late + 1], panels, held_tiles, total, basis, spread)

    tables = [table]
    for hop in range(group_count - 1, 0, -1):
        tables.append(exchange(table, "col", hop))

    gradient = pl.pallas_call(
        functools.partial(gradient_kernel, len(tables)),
        out_shape=jax.ShapeDtypeStruct((block_count, node_count), F32),
        in_specs=[VMEM_SPEC] * (len(tables) + 4),
        out_specs=VMEM_SPEC,
        compiler_params=params(),
        name="gradient_stage",
    )(*tables, basis, spread, powers, crosses)
    return (field, gradient)


def solution(mesh):
    in_specs = (
        P(("row", "col"), None, None),
        P(("row", "col"), None, None),
        P(("row", "col")),
        P(("row", "col")),
        P(("row", "col"), None, None),
        P(("row", "col"), None),
        P(("row", "col"), None),
        P(("row", "col")),
    )
    out_specs = (P(("row", "col"), None, None), P(("row", "col"), None))
    return jax.shard_map(shards, mesh=mesh, in_specs=in_specs, out_specs=out_specs, check_vma=False)
```

```python
import functools

import jax
import jax.numpy as jnp
from jax import lax
from jax.experimental import pallas as pl
from jax.experimental.pallas import tpu as pltpu
from jax.sharding import PartitionSpec as P

PD = 4
EPSILON = 1e-05
UNROLL = 4
MOMENTS = 8
F32 = jnp.float32
BF16 = jnp.bfloat16
VMEM_LIMIT = 8 << 20
LOAD_LIMIT = 44 << 20
COPIES = 8

VMEM_SPEC = pl.BlockSpec(memory_space=pltpu.VMEM)
SMEM_SPEC = pl.BlockSpec(memory_space=pltpu.SMEM)
HBM_SPEC = pl.BlockSpec(memory_space=pltpu.HBM)


def params(limit=VMEM_LIMIT):
    return pltpu.CompilerParams(vmem_limit_bytes=limit)


def parts_of(values, count):
    parts = []
    for _ in range(count - 1):
        part = values.astype(BF16)
        parts.append(part)
        values = values - part.astype(F32)
    parts.append(values.astype(BF16))
    return parts


def dot(left, right, transposed=False):
    axes = (((1,), (1 if transposed else 0,)), ((), ()))
    return lax.dot_general(left, right, axes, preferred_element_type=F32)


def dot_near_exact(left, right, transposed=False):
    left_high, left_low = parts_of(left, 2)
    right_high, right_low = parts_of(right, 2)
    return dot(left_high, right_high, transposed) + (
        dot(left_high, right_low, transposed) + dot(left_low, right_high, transposed)
    )


def block_mask(block_count, freq_count):
    shape = (block_count, block_count * freq_count)
    rows = lax.broadcasted_iota(jnp.int32, shape, 0)
    columns = lax.broadcasted_iota(jnp.int32, shape, 1)
    return (columns // freq_count == rows).astype(F32)


def fill_panels(sources, held):
    depth = sources[0].shape[0]
    for index, source in enumerate(sources):
        held[index * depth : (index + 1) * depth] = source[...]
    held[len(sources) * depth] = jnp.zeros(held.shape[1:], held.dtype)


def add_stage(stage, region, plan, held, tiles, total):
    count = plan[3 * (plan.shape[0] // 4) + stage]
    add_groups(stage, region, 0, (count + UNROLL - 1) // UNROLL, plan, held, tiles, total)


def add_groups(stage, region, begin, end, plan, held, tiles, total):
    width = plan.shape[0] // 4
    start = stage * region

    def body(step, carry):
        base = start + step * UNROLL
        images = [
            dot(held[plan[width + base + lane]], tiles[plan[base + lane]])
            for lane in range(UNROLL)
        ]
        for lane in range(UNROLL):
            target = plan[2 * width + base + lane]
            total[target] += images[lane]
        return carry

    lax.fori_loop(begin, end, body, 0)


def load_kernel(
    stages, region, freq_count, src, dst, owner, slot, panels, place, areas, tiles,
    plan, held_tiles, total, basis, spread, held, sems,
):
    tile_count = tiles.shape[0]
    edges = [tile_count * i // COPIES for i in range(COPIES + 1)]
    copies = []
    for i in range(COPIES):
        span = pl.ds(edges[i], edges[i + 1] - edges[i])
        copies.append(pltpu.make_async_copy(tiles.at[span], held_tiles.at[span], sems.at[i]))
    for copy in copies:
        copy.start()
    block_count = areas.shape[0]
    width = plan.shape[0] // 4
    me = lax.axis_index("row")

    def place_tile(t, counts):
        source = src[t]
        hop = (source // block_count) ^ me
        target, here, row = jnp.int32(0), [], jnp.int32(0)
        for stage, hops in enumerate(stages):
            inside = hop == hops[0]
            for index, other in enumerate(hops[1:], 1):
                inside = inside | (hop == other)
                row = jnp.where(hop == other, index, row)
            target = jnp.where(inside, stage * region + counts[stage], target)
            here.append(inside)
        plan[target] = t
        plan[width + target] = row * block_count + source % block_count
        plan[2 * width + target] = dst[t]
        return tuple(count + inside.astype(jnp.int32) for count, inside in zip(counts, here))

    counts = (jnp.int32(0),) * len(stages)
    ready = []
    for i in range(COPIES):
        counts = lax.fori_loop(edges[i], edges[i + 1], place_tile, counts)
        ready.append(counts[0] // UNROLL)
    ready[-1] = (counts[0] + UNROLL - 1) // UNROLL
    for stage, hops in enumerate(stages):
        plan[3 * width + stage] = counts[stage]
        loaded = plan[stage * region]
        for lane in range(UNROLL):
            position = stage * region + counts[stage] + lane
            plan[position] = loaded
            plan[width + position] = len(hops) * block_count
            plan[2 * width + position] = 0
    total[...] = jnp.zeros_like(total)
    fill_panels([panels], held)
    nx, ny, nz, px, py, pz = [place[i] for i in range(6)]
    weight = areas[...]
    rows = [nx, ny, nz, py * nz - pz * ny, pz * nx - px * nz, px * ny - py * nx]
    for index, row in enumerate(rows):
        basis[index * block_count : (index + 1) * block_count] = weight * row
    for index in range(len(rows), MOMENTS):
        basis[index * block_count : (index + 1) * block_count] = weight
    shape = (freq_count, spread.shape[1])
    lanes = lax.broadcasted_iota(jnp.int32, shape, 1)
    same = lanes % freq_count == lax.broadcasted_iota(jnp.int32, shape, 0)
    for block in range(block_count):
        particle = owner[block] * PD + slot[block]
        chosen = same & (lanes // freq_count == particle)
        spread[block * freq_count : (block + 1) * freq_count] = jnp.where(
            chosen, 1.0, 0.0
        ).astype(BF16)
    begin = jnp.int32(0)
    for copy, end in zip(copies, ready):
        copy.wait()
        add_groups(0, region, begin, end, plan, held, held_tiles, total)
        begin = end


def near_kernel(stage, region, count, plan, *refs):
    sources = refs[:count]
    tiles, start, total, held = refs[count:]
    fill_panels(sources, held)
    add_stage(stage, region, plan, held, tiles, total)


def field_kernel(stage, region, count, plan, *refs):
    sources = refs[:count]
    panels, tiles, start, basis, spread = refs[count : count + 5]
    total, field, table, powers, crosses, held = refs[count + 5 :]
    block_count, rows_twice, node_count = panels.shape
    freq_count = rows_twice // 2
    fill_panels(sources, held)
    add_stage(stage, region, plan, held, tiles, total)
    for block in range(block_count):
        image = total[block]
        incident = panels[block].astype(F32)
        real_in, imag_in = incident[:freq_count], incident[freq_count:]
        real = 0.5 * real_in + (
            image[:freq_count, :node_count] - image[freq_count:, node_count:]
        )
        imag = 0.5 * imag_in + (
            image[:freq_count, node_count:] + image[freq_count:, :node_count]
        )
        field[block, :freq_count] = real
        field[block, freq_count:] = imag
        span = slice(block * freq_count, (block + 1) * freq_count)
        powers[span] = real * real + imag * imag
        crosses[span] = real_in * real + imag_in * imag
    last = (MOMENTS - 1) * block_count
    first_moments = dot_near_exact(basis[:last], powers[...], True)
    last_moment = dot_near_exact(basis[last:], crosses[...], True)
    mask = block_mask(block_count, freq_count)
    pieces = [
        jnp.sum(mask * first_moments[k * block_count : (k + 1) * block_count], axis=0, keepdims=True)
        for k in range(MOMENTS - 1)
    ]
    pieces.append(jnp.sum(mask * last_moment, axis=0, keepdims=True))
    moments = jnp.concatenate(pieces, axis=0)
    joined = dot(jnp.concatenate(parts_of(moments, 3), axis=0), spread[...])
    table[...] = joined[:MOMENTS] + (joined[MOMENTS : 2 * MOMENTS] + joined[2 * MOMENTS :])


def gradient_kernel(count, *refs):
    tables = refs[:count]
    basis, spread, powers, crosses, gradient = refs[count:]
    block_count = gradient.shape[0]
    freq_count = powers.shape[0] // block_count
    summed = tables[0][...]
    for table in tables[1:]:
        summed = summed + table[...]
    joined = dot(jnp.concatenate(parts_of(summed, 3), axis=0), spread[...], True)
    totals = joined[:MOMENTS] + (joined[MOMENTS : 2 * MOMENTS] + joined[2 * MOMENTS :])
    mask = block_mask(block_count, freq_count)
    squares = jnp.sum(totals * totals, axis=0, keepdims=True)
    mean = jnp.sum(mask * squares, axis=1, keepdims=True) / (MOMENTS * freq_count)
    scale = lax.rsqrt(mean + EPSILON) / freq_count
    spots = [mask * totals[k : k + 1] for k in range(MOMENTS)]
    first_terms = dot_near_exact(jnp.concatenate(spots[:-1], axis=0), powers[...])
    last_term = dot_near_exact(spots[-1], crosses[...])
    result = basis[(MOMENTS - 1) * block_count :] * last_term
    for k in range(MOMENTS - 1):
        span = slice(k * block_count, (k + 1) * block_count)
        result = result + basis[span] * first_terms[span]
    gradient[...] = result * scale


def exchange(values, axis, hop):
    pairs = [(i, i ^ hop) for i in range(lax.axis_size(axis))]
    return lax.ppermute(values, axis, pairs)


def shards(panels, tiles, tile_dst, tile_src, geometry, areas, block_owner, block_slot):
    block_count, rows_twice, node_count = panels.shape
    freq_count = rows_twice // 2
    tile_count = tiles.shape[0]
    row_count = lax.axis_size("row")
    group_count = lax.axis_size("col")
    particle_count = group_count * PD
    first, late = row_count // 2, row_count - 2
    others = [hop for hop in range(2, row_count, 2) if hop not in (first, late)]
    stages = (
        [0],
        [first, *others],
        [first + 1, *[hop + 1 for hop in others], late, 1],
        [late + 1],
    )
    region = tile_count + UNROLL
    width = -(-(len(stages) * region) // 128) * 128
    image_shape = (block_count, rows_twice, 2 * node_count)
    basis_shape = (MOMENTS * block_count, node_count)
    spread_shape = (block_count * freq_count, particle_count * freq_count)
    power_shape = (block_count * freq_count, node_count)
    table_shape = (MOMENTS, particle_count * freq_count)

    def held(stage):
        return pltpu.VMEM((len(stages[stage]) * block_count + 1, rows_twice, node_count), BF16)

    hops = {0: panels}
    for hop in [first, *others, late, 1]:
        hops[hop] = exchange(panels, "row", hop)

    plan, held_tiles, total, basis, spread = pl.pallas_call(
        functools.partial(load_kernel, stages, region, freq_count),
        out_shape=(
            pltpu.SMEM((4 * width,), jnp.int32),
            pltpu.VMEM(tiles.shape, tiles.dtype),
            pltpu.VMEM(image_shape, F32),
            pltpu.VMEM(basis_shape, F32),
            pltpu.VMEM(spread_shape, BF16),
        ),
        in_specs=[SMEM_SPEC] * 4 + [VMEM_SPEC] * 3 + [HBM_SPEC],
        out_specs=(SMEM_SPEC,) + (VMEM_SPEC,) * 4,
        scratch_shapes=[held(0), pltpu.SemaphoreType.DMA((COPIES,))],
        compiler_params=params(LOAD_LIMIT),
        cost_estimate=pl.CostEstimate(flops=0, bytes_accessed=tiles.size * 2, transcendentals=0),
        name="load_stage",
    )(
        tile_src,
        tile_dst,
        block_owner[:, 0],
        block_slot,
        panels,
        jnp.transpose(geometry, (1, 0, 2)),
        areas,
        tiles,
    )

    def near(stage, total):
        sources = [hops[hop] for hop in stages[stage]]
        return pl.pallas_call(
            functools.partial(near_kernel, stage, region, len(sources)),
            out_shape=pltpu.VMEM(image_shape, F32),
            in_specs=[SMEM_SPEC] + [VMEM_SPEC] * (len(sources) + 2),
            out_specs=VMEM_SPEC,
            scratch_shapes=[held(stage)],
            input_output_aliases={len(sources) + 2: 0},
            compiler_params=params(),
            name="near_stage",
        )(plan, *sources, held_tiles, total)

    for hop in [first, *others]:
        hops[hop], total = lax.optimization_barrier((hops[hop], total))
        hops[hop + 1] = exchange(hops[hop], "row", 1)
    total = near(1, total)
    hops[late], total = lax.optimization_barrier((hops[late], total))
    hops[late + 1] = exchange(hops[late], "row", 1)
    total = near(2, total)

    total, field, table, powers, crosses = pl.pallas_call(
        functools.partial(field_kernel, 3, region, 1),
        out_shape=(
            pltpu.VMEM(image_shape, F32),
            pltpu.VMEM(panels.shape, F32),
            pltpu.VMEM(table_shape, F32),
            pltpu.VMEM(power_shape, F32),
            pltpu.VMEM(power_shape, F32),
        ),
        in_specs=[SMEM_SPEC] + [VMEM_SPEC] * 6,
        out_specs=(VMEM_SPEC,) * 5,
        scratch_shapes=[held(3)],
        input_output_aliases={4: 0},
        compiler_params=params(),
        name="field_stage",
    )(plan, hops[late + 1], panels, held_tiles, total, basis, spread)

    tables = [table]
    for hop in range(1, group_count):
        tables.append(exchange(table, "col", hop))

    gradient = pl.pallas_call(
        functools.partial(gradient_kernel, len(tables)),
        out_shape=jax.ShapeDtypeStruct((block_count, node_count), F32),
        in_specs=[VMEM_SPEC] * (len(tables) + 4),
        out_specs=VMEM_SPEC,
        compiler_params=params(),
        name="gradient_stage",
    )(*tables, basis, spread, powers, crosses)
    return (field, gradient)


def solution(mesh):
    in_specs = (
        P(("row", "col"), None, None),
        P(("row", "col"), None, None),
        P(("row", "col")),
        P(("row", "col")),
        P(("row", "col"), None, None),
        P(("row", "col"), None),
        P(("row", "col"), None),
        P(("row", "col")),
    )
    out_specs = (P(("row", "col"), None, None), P(("row", "col"), None))
    return jax.shard_map(shards, mesh=mesh, in_specs=in_specs, out_specs=out_specs, check_vma=False)
```

```python
import functools

import jax
import jax.numpy as jnp
from jax import lax
from jax.experimental import pallas as pl
from jax.experimental.pallas import tpu as pltpu
from jax.sharding import PartitionSpec as P

PD = 4
EPSILON = 1e-05
UNROLL = 4
MOMENTS = 8
SMALL = 1 << 16
F32 = jnp.float32
BF16 = jnp.bfloat16
VMEM_LIMIT = 8 << 20
EARLY_LIMIT = 44 << 20

VMEM_SPEC = pl.BlockSpec(memory_space=pltpu.VMEM)
SMEM_SPEC = pl.BlockSpec(memory_space=pltpu.SMEM)
HBM_SPEC = pl.BlockSpec(memory_space=pltpu.HBM)


def cost(size):
    return pl.CostEstimate(flops=0, bytes_accessed=size, transcendentals=0)


def params(limit=VMEM_LIMIT):
    return pltpu.CompilerParams(vmem_limit_bytes=limit)


def parts_of(values, count):
    parts = []
    for _ in range(count - 1):
        part = values.astype(BF16)
        parts.append(part)
        values = values - part.astype(F32)
    parts.append(values.astype(BF16))
    return parts


def dot(left, right, transposed=False):
    axes = (((1,), (1 if transposed else 0,)), ((), ()))
    return lax.dot_general(left, right, axes, preferred_element_type=F32)


def dot_near_exact(left, right, transposed=False):
    left_high, left_low = parts_of(left, 2)
    right_high, right_low = parts_of(right, 2)
    return dot(left_high, right_high, transposed) + (
        dot(left_high, right_low, transposed) + dot(left_low, right_high, transposed)
    )


def block_mask(block_count, freq_count):
    shape = (block_count, block_count * freq_count)
    rows = lax.broadcasted_iota(jnp.int32, shape, 0)
    columns = lax.broadcasted_iota(jnp.int32, shape, 1)
    return (columns // freq_count == rows).astype(F32)


def fill_panels(sources, held):
    depth = sources[0].shape[0]
    for index, source in enumerate(sources):
        held[index * depth : (index + 1) * depth] = source[...]
    held[len(sources) * depth] = jnp.zeros(held.shape[1:], held.dtype)


def add_stage(stage, region, plan, held, tiles, total):
    count = plan[3 * (plan.shape[0] // 4) + stage]
    add_groups(stage, region, 0, (count + UNROLL - 1) // UNROLL, plan, held, tiles, total)


def add_groups(stage, region, begin, end, plan, held, tiles, total):
    width = plan.shape[0] // 4
    start = stage * region

    def body(step, carry):
        base = start + step * UNROLL
        images = [
            dot(held[plan[width + base + lane]], tiles[plan[base + lane]])
            for lane in range(UNROLL)
        ]
        for lane in range(UNROLL):
            target = plan[2 * width + base + lane]
            total[target] += images[lane]
        return carry

    lax.fori_loop(begin, end, body, 0)


def early_kernel(tiles, token):
    token[...] = jnp.zeros_like(token)


def plan_kernel(stages, region, freq_count, table, src, dst, owner, slot, token, plan, total, spread):
    block_count = owner.shape[0]
    width = plan.shape[0] // 4
    row_count = lax.axis_size("row")
    me = lax.axis_index("row")

    def place_tile(t, counts):
        source = src[t]
        found = table[(source // block_count) ^ me]
        target = jnp.int32(0)
        for stage in range(len(stages)):
            target = jnp.where(found // row_count == stage, stage * region + counts[stage], target)
        plan[target] = t
        plan[width + target] = found % row_count * block_count + source % block_count
        plan[2 * width + target] = dst[t]
        return tuple(
            count + (found // row_count == stage).astype(jnp.int32)
            for stage, count in enumerate(counts)
        )

    counts = lax.fori_loop(0, src.shape[0], place_tile, (jnp.int32(0),) * len(stages))
    for stage, held in enumerate(stages):
        plan[3 * width + stage] = counts[stage]
        for lane in range(UNROLL):
            position = stage * region + counts[stage] + lane
            plan[position] = 0
            plan[width + position] = len(held) * block_count
            plan[2 * width + position] = 0
    total[...] = jnp.zeros_like(total)
    shape = (freq_count, spread.shape[1])
    lanes = lax.broadcasted_iota(jnp.int32, shape, 1)
    same = lanes % freq_count == lax.broadcasted_iota(jnp.int32, shape, 0)
    for block in range(block_count):
        particle = owner[block] * PD + slot[block]
        chosen = same & (lanes // freq_count == particle)
        spread[block * freq_count : (block + 1) * freq_count] = jnp.where(
            chosen, 1.0, 0.0
        ).astype(BF16)


def basis_kernel(place, areas, basis):
    block_count = areas.shape[0]
    nx, ny, nz, px, py, pz = [place[i] for i in range(6)]
    weight = areas[...]
    rows = [nx, ny, nz, py * nz - pz * ny, pz * nx - px * nz, px * ny - py * nx]
    for index, row in enumerate(rows):
        basis[index * block_count : (index + 1) * block_count] = weight * row
    for index in range(len(rows), MOMENTS):
        basis[index * block_count : (index + 1) * block_count] = weight


def near_kernel(stage, region, count, plan, *refs):
    sources = refs[:count]
    tiles, start, total, held = refs[count:]
    fill_panels(sources, held)
    add_stage(stage, region, plan, held, tiles, total)


def field_kernel(stage, region, count, plan, *refs):
    sources = refs[:count]
    panels, tiles, start, basis, spread = refs[count : count + 5]
    total, field, table, powers, crosses, held = refs[count + 5 :]
    block_count, rows_twice, node_count = panels.shape
    freq_count = rows_twice // 2
    fill_panels(sources, held)
    add_stage(stage, region, plan, held, tiles, total)
    for block in range(block_count):
        image = total[block]
        incident = panels[block].astype(F32)
        real_in, imag_in = incident[:freq_count], incident[freq_count:]
        real = 0.5 * real_in + (
            image[:freq_count, :node_count] - image[freq_count:, node_count:]
        )
        imag = 0.5 * imag_in + (
            image[:freq_count, node_count:] + image[freq_count:, :node_count]
        )
        field[block, :freq_count] = real
        field[block, freq_count:] = imag
        span = slice(block * freq_count, (block + 1) * freq_count)
        powers[span] = real * real + imag * imag
        crosses[span] = real_in * real + imag_in * imag
    last = (MOMENTS - 1) * block_count
    first_moments = dot_near_exact(basis[:last], powers[...], True)
    last_moment = dot_near_exact(basis[last:], crosses[...], True)
    mask = block_mask(block_count, freq_count)
    pieces = [
        jnp.sum(mask * first_moments[k * block_count : (k + 1) * block_count], axis=0, keepdims=True)
        for k in range(MOMENTS - 1)
    ]
    pieces.append(jnp.sum(mask * last_moment, axis=0, keepdims=True))
    moments = jnp.concatenate(pieces, axis=0)
    joined = dot(jnp.concatenate(parts_of(moments, 3), axis=0), spread[...])
    table[...] = joined[:MOMENTS] + (joined[MOMENTS : 2 * MOMENTS] + joined[2 * MOMENTS :])


def gradient_kernel(count, *refs):
    tables = refs[:count]
    basis, spread, powers, crosses, gradient = refs[count:]
    block_count = gradient.shape[0]
    freq_count = powers.shape[0] // block_count
    summed = tables[0][...]
    for table in tables[1:]:
        summed = summed + table[...]
    joined = dot(jnp.concatenate(parts_of(summed, 3), axis=0), spread[...], True)
    totals = joined[:MOMENTS] + (joined[MOMENTS : 2 * MOMENTS] + joined[2 * MOMENTS :])
    mask = block_mask(block_count, freq_count)
    squares = jnp.sum(totals * totals, axis=0, keepdims=True)
    mean = jnp.sum(mask * squares, axis=1, keepdims=True) / (MOMENTS * freq_count)
    scale = lax.rsqrt(mean + EPSILON) / freq_count
    spots = [mask * totals[k : k + 1] for k in range(MOMENTS)]
    first_terms = dot_near_exact(jnp.concatenate(spots[:-1], axis=0), powers[...])
    last_term = dot_near_exact(spots[-1], crosses[...])
    result = basis[(MOMENTS - 1) * block_count :] * last_term
    for k in range(MOMENTS - 1):
        span = slice(k * block_count, (k + 1) * block_count)
        result = result + basis[span] * first_terms[span]
    gradient[...] = result * scale


def exchange(values, axis, hop):
    pairs = [(i, i ^ hop) for i in range(lax.axis_size(axis))]
    return lax.ppermute(values, axis, pairs)


def shards(panels, tiles, tile_dst, tile_src, geometry, areas, block_owner, block_slot):
    block_count, rows_twice, node_count = panels.shape
    freq_count = rows_twice // 2
    tile_count = tiles.shape[0]
    row_count = lax.axis_size("row")
    group_count = lax.axis_size("col")
    particle_count = group_count * PD
    image_shape = (block_count, rows_twice, 2 * node_count)
    basis_shape = (MOMENTS * block_count, node_count)
    spread_shape = (block_count * freq_count, particle_count * freq_count)
    power_shape = (block_count * freq_count, node_count)
    table_shape = (MOMENTS, particle_count * freq_count)
    region = tile_count + UNROLL

    token = pl.pallas_call(
        early_kernel,
        out_shape=pltpu.VMEM((8, 128), F32),
        in_specs=[HBM_SPEC],
        out_specs=VMEM_SPEC,
        compiler_params=params(EARLY_LIMIT),
        cost_estimate=cost(4 * tiles.size),
        name="early_stage",
    )(tiles)

    first, late = row_count // 2, row_count - 2
    middle = [first, *[hop for hop in range(2, row_count, 2) if hop not in (first, late)]]
    stages = ([0], [*middle, 1], [*[hop + 1 for hop in middle], late], [late + 1])
    places = {
        hop: stage * row_count + index
        for stage, hops in enumerate(stages)
        for index, hop in enumerate(hops)
    }
    table = jnp.array([places[hop] for hop in range(row_count)], jnp.int32)
    width = -(-(len(stages) * region) // 128) * 128

    arrived = {0: panels}
    token, out = lax.optimization_barrier((token, panels))
    for hop in [*middle, late, 1]:
        arrived[hop] = exchange(out, "row", hop)

    plan, total, spread = pl.pallas_call(
        functools.partial(plan_kernel, stages, region, freq_count),
        out_shape=(
            pltpu.SMEM((4 * width,), jnp.int32),
            pltpu.VMEM(image_shape, F32),
            pltpu.VMEM(spread_shape, BF16),
        ),
        in_specs=[SMEM_SPEC] * 5 + [VMEM_SPEC],
        out_specs=(SMEM_SPEC,) + (VMEM_SPEC,) * 2,
        compiler_params=params(),
        cost_estimate=cost(4 * tiles.size),
        name="plan_stage",
    )(table, tile_src, tile_dst, block_owner[:, 0], block_slot, token)

    def near(stage, total):
        sources = [arrived[hop] for hop in stages[stage]]
        scratch = pltpu.VMEM((len(sources) * block_count + 1, rows_twice, node_count), BF16)
        return pl.pallas_call(
            functools.partial(near_kernel, stage, region, len(sources)),
            out_shape=pltpu.VMEM(image_shape, F32),
            in_specs=[SMEM_SPEC] + [VMEM_SPEC] * (len(sources) + 2),
            out_specs=VMEM_SPEC,
            scratch_shapes=[scratch],
            input_output_aliases={len(sources) + 2: 0},
            compiler_params=params(),
            cost_estimate=cost(SMALL),
            name="near_stage",
        )(plan, *sources, tiles, total)

    def forward(hop, total):
        arrived[hop], total = lax.optimization_barrier((arrived[hop], total))
        arrived[hop + 1] = exchange(arrived[hop], "row", 1)
        return total

    total = near(0, total)
    for hop in middle:
        total = forward(hop, total)
    total = near(1, total)
    weights, total = lax.optimization_barrier((areas, total))
    basis = pl.pallas_call(
        basis_kernel,
        out_shape=pltpu.VMEM(basis_shape, F32),
        in_specs=[VMEM_SPEC] * 2,
        out_specs=VMEM_SPEC,
        compiler_params=params(),
        cost_estimate=cost(SMALL),
        name="basis_stage",
    )(jnp.transpose(geometry, (1, 0, 2)), weights)
    total = forward(late, total)
    total = near(2, total)

    total, field, table, powers, crosses = pl.pallas_call(
        functools.partial(field_kernel, 3, region, 1),
        out_shape=(
            pltpu.VMEM(image_shape, F32),
            pltpu.VMEM(panels.shape, F32),
            pltpu.VMEM(table_shape, F32),
            pltpu.VMEM(power_shape, F32),
            pltpu.VMEM(power_shape, F32),
        ),
        in_specs=[SMEM_SPEC] + [VMEM_SPEC] * 6,
        out_specs=(VMEM_SPEC,) * 5,
        scratch_shapes=[pltpu.VMEM((block_count + 1, rows_twice, node_count), BF16)],
        input_output_aliases={4: 0},
        compiler_params=params(),
        cost_estimate=cost(SMALL),
        name="field_stage",
    )(plan, arrived[late + 1], panels, tiles, total, basis, spread)

    tables = [table]
    for distance in range(1, group_count):
        tables.append(exchange(table, "col", distance))

    gradient = pl.pallas_call(
        functools.partial(gradient_kernel, len(tables)),
        out_shape=jax.ShapeDtypeStruct((block_count, node_count), F32),
        in_specs=[VMEM_SPEC] * (len(tables) + 4),
        out_specs=VMEM_SPEC,
        compiler_params=params(),
        cost_estimate=cost(SMALL),
        name="gradient_stage",
    )(*tables, basis, spread, powers, crosses)
    return (field, gradient)


def solution(mesh):
    in_specs = (
        P(("row", "col"), None, None),
        P(("row", "col"), None, None),
        P(("row", "col")),
        P(("row", "col")),
        P(("row", "col"), None, None),
        P(("row", "col"), None),
        P(("row", "col"), None),
        P(("row", "col")),
    )
    out_specs = (P(("row", "col"), None, None), P(("row", "col"), None))
    return jax.shard_map(shards, mesh=mesh, in_specs=in_specs, out_specs=out_specs, check_vma=False)
```

```python
import functools

import jax
import jax.numpy as jnp
from jax import lax
from jax.experimental import pallas as pl
from jax.experimental.pallas import tpu as pltpu
from jax.sharding import PartitionSpec as P

PD = 4
EPSILON = 1e-05
UNROLL = 8
MOMENTS = 8
SMALL = 1 << 16
F32 = jnp.float32
BF16 = jnp.bfloat16
VMEM_LIMIT = 8 << 20
EARLY_LIMIT = 44 << 20

VMEM_SPEC = pl.BlockSpec(memory_space=pltpu.VMEM)
SMEM_SPEC = pl.BlockSpec(memory_space=pltpu.SMEM)
HBM_SPEC = pl.BlockSpec(memory_space=pltpu.HBM)


def cost(size):
    return pl.CostEstimate(flops=0, bytes_accessed=size, transcendentals=0)


def params(limit=VMEM_LIMIT):
    return pltpu.CompilerParams(vmem_limit_bytes=limit)


def parts_of(values, count):
    parts = []
    for _ in range(count - 1):
        part = values.astype(BF16)
        parts.append(part)
        values = values - part.astype(F32)
    parts.append(values.astype(BF16))
    return parts


def dot(left, right, transposed=False):
    axes = (((1,), (1 if transposed else 0,)), ((), ()))
    return lax.dot_general(left, right, axes, preferred_element_type=F32)


def dot_near_exact(left, right, transposed=False):
    left_high, left_low = parts_of(left, 2)
    right_high, right_low = parts_of(right, 2)
    return dot(left_high, right_high, transposed) + (
        dot(left_high, right_low, transposed) + dot(left_low, right_high, transposed)
    )


def block_mask(block_count, freq_count):
    shape = (block_count, block_count * freq_count)
    rows = lax.broadcasted_iota(jnp.int32, shape, 0)
    columns = lax.broadcasted_iota(jnp.int32, shape, 1)
    return (columns // freq_count == rows).astype(F32)


def fill_panels(sources, held):
    depth = sources[0].shape[0]
    for index, source in enumerate(sources):
        held[index * depth : (index + 1) * depth] = source[...]
    held[len(sources) * depth] = jnp.zeros(held.shape[1:], held.dtype)


def add_stage(stage, region, plan, held, tiles, total):
    width = plan.shape[0] // 4
    count = plan[3 * width + stage]
    whole = count // UNROLL

    def add_group(base, size):
        images = [
            dot(held[plan[width + base + lane]], tiles[plan[base + lane]])
            for lane in range(size)
        ]
        for lane in range(size):
            target = plan[2 * width + base + lane]
            total[target] += images[lane]

    def body(step, carry):
        add_group(stage * region + step * UNROLL, UNROLL)
        return carry

    lax.fori_loop(0, whole, body, 0)
    left = count - whole * UNROLL
    for size in range(2, UNROLL + 1, 2):

        @pl.when((left > size - 2) & (left <= size))
        def _(size=size):
            add_group(stage * region + whole * UNROLL, size)


def early_kernel(tiles, token):
    token[...] = jnp.zeros_like(token)


def plan_kernel(stages, region, freq_count, table, src, dst, owner, slot, token, plan, total, spread):
    block_count = owner.shape[0]
    width = plan.shape[0] // 4
    row_count = lax.axis_size("row")
    me = lax.axis_index("row")

    def place_tile(t, counts):
        source = src[t]
        found = table[(source // block_count) ^ me]
        target = jnp.int32(0)
        for stage in range(len(stages)):
            target = jnp.where(found // row_count == stage, stage * region + counts[stage], target)
        plan[target] = t
        plan[width + target] = found % row_count * block_count + source % block_count
        plan[2 * width + target] = dst[t]
        return tuple(
            count + (found // row_count == stage).astype(jnp.int32)
            for stage, count in enumerate(counts)
        )

    counts = lax.fori_loop(0, src.shape[0], place_tile, (jnp.int32(0),) * len(stages))
    for stage, held in enumerate(stages):
        plan[3 * width + stage] = counts[stage]
        for lane in range(UNROLL):
            position = stage * region + counts[stage] + lane
            plan[position] = 0
            plan[width + position] = len(held) * block_count
            plan[2 * width + position] = 0
    total[...] = jnp.zeros_like(total)
    shape = (freq_count, spread.shape[1])
    lanes = lax.broadcasted_iota(jnp.int32, shape, 1)
    same = lanes % freq_count == lax.broadcasted_iota(jnp.int32, shape, 0)
    for block in range(block_count):
        particle = owner[block] * PD + slot[block]
        chosen = same & (lanes // freq_count == particle)
        spread[block * freq_count : (block + 1) * freq_count] = jnp.where(
            chosen, 1.0, 0.0
        ).astype(BF16)


def basis_kernel(place, areas, basis):
    block_count = areas.shape[0]
    nx, ny, nz, px, py, pz = [place[i] for i in range(6)]
    weight = areas[...]
    rows = [nx, ny, nz, py * nz - pz * ny, pz * nx - px * nz, px * ny - py * nx]
    for index, row in enumerate(rows):
        basis[index * block_count : (index + 1) * block_count] = weight * row
    for index in range(len(rows), MOMENTS):
        basis[index * block_count : (index + 1) * block_count] = weight


def near_kernel(stage, region, count, plan, *refs):
    sources = refs[:count]
    tiles, start, total, held = refs[count:]
    fill_panels(sources, held)
    add_stage(stage, region, plan, held, tiles, total)


def field_kernel(stage, region, count, plan, *refs):
    sources = refs[:count]
    panels, tiles, start, basis, spread = refs[count : count + 5]
    total, field, table, powers, crosses, held = refs[count + 5 :]
    block_count, rows_twice, node_count = panels.shape
    freq_count = rows_twice // 2
    fill_panels(sources, held)
    add_stage(stage, region, plan, held, tiles, total)
    for block in range(block_count):
        image = total[block]
        incident = panels[block].astype(F32)
        real_in, imag_in = incident[:freq_count], incident[freq_count:]
        real = 0.5 * real_in + (
            image[:freq_count, :node_count] - image[freq_count:, node_count:]
        )
        imag = 0.5 * imag_in + (
            image[:freq_count, node_count:] + image[freq_count:, :node_count]
        )
        field[block, :freq_count] = real
        field[block, freq_count:] = imag
        span = slice(block * freq_count, (block + 1) * freq_count)
        powers[span] = real * real + imag * imag
        crosses[span] = real_in * real + imag_in * imag
    last = (MOMENTS - 1) * block_count
    first_moments = dot_near_exact(basis[:last], powers[...], True)
    last_moment = dot_near_exact(basis[last:], crosses[...], True)
    mask = block_mask(block_count, freq_count)
    pieces = [
        jnp.sum(mask * first_moments[k * block_count : (k + 1) * block_count], axis=0, keepdims=True)
        for k in range(MOMENTS - 1)
    ]
    pieces.append(jnp.sum(mask * last_moment, axis=0, keepdims=True))
    moments = jnp.concatenate(pieces, axis=0)
    joined = dot(jnp.concatenate(parts_of(moments, 3), axis=0), spread[...])
    table[...] = joined[:MOMENTS] + (joined[MOMENTS : 2 * MOMENTS] + joined[2 * MOMENTS :])


def gradient_kernel(count, *refs):
    tables = refs[:count]
    basis, spread, powers, crosses, gradient = refs[count:]
    block_count = gradient.shape[0]
    freq_count = powers.shape[0] // block_count
    summed = tables[0][...]
    for table in tables[1:]:
        summed = summed + table[...]
    joined = dot(jnp.concatenate(parts_of(summed, 3), axis=0), spread[...], True)
    totals = joined[:MOMENTS] + (joined[MOMENTS : 2 * MOMENTS] + joined[2 * MOMENTS :])
    mask = block_mask(block_count, freq_count)
    squares = jnp.sum(totals * totals, axis=0, keepdims=True)
    mean = jnp.sum(mask * squares, axis=1, keepdims=True) / (MOMENTS * freq_count)
    scale = lax.rsqrt(mean + EPSILON) / freq_count
    spots = [mask * totals[k : k + 1] for k in range(MOMENTS)]
    first_terms = dot_near_exact(jnp.concatenate(spots[:-1], axis=0), powers[...])
    last_term = dot_near_exact(spots[-1], crosses[...])
    result = basis[(MOMENTS - 1) * block_count :] * last_term
    for k in range(MOMENTS - 1):
        span = slice(k * block_count, (k + 1) * block_count)
        result = result + basis[span] * first_terms[span]
    gradient[...] = result * scale


def exchange(values, axis, hop):
    pairs = [(i, i ^ hop) for i in range(lax.axis_size(axis))]
    return lax.ppermute(values, axis, pairs)


def shards(panels, tiles, tile_dst, tile_src, geometry, areas, block_owner, block_slot):
    block_count, rows_twice, node_count = panels.shape
    freq_count = rows_twice // 2
    tile_count = tiles.shape[0]
    row_count = lax.axis_size("row")
    group_count = lax.axis_size("col")
    particle_count = group_count * PD
    image_shape = (block_count, rows_twice, 2 * node_count)
    basis_shape = (MOMENTS * block_count, node_count)
    spread_shape = (block_count * freq_count, particle_count * freq_count)
    power_shape = (block_count * freq_count, node_count)
    table_shape = (MOMENTS, particle_count * freq_count)
    region = tile_count + UNROLL

    token = pl.pallas_call(
        early_kernel,
        out_shape=pltpu.VMEM((8, 128), F32),
        in_specs=[HBM_SPEC],
        out_specs=VMEM_SPEC,
        compiler_params=params(EARLY_LIMIT),
        cost_estimate=cost(4 * tiles.size),
        name="early_stage",
    )(tiles)

    first, late = row_count // 2, row_count - 2
    middle = [first, *[hop for hop in range(2, row_count, 2) if hop not in (first, late)]]
    stages = ([0], [*middle, 1], [*[hop + 1 for hop in middle], late], [late + 1])
    places = {
        hop: stage * row_count + index
        for stage, hops in enumerate(stages)
        for index, hop in enumerate(hops)
    }
    table = jnp.array([places[hop] for hop in range(row_count)], jnp.int32)
    width = -(-(len(stages) * region) // 128) * 128

    arrived = {0: panels}
    token, out = lax.optimization_barrier((token, panels))
    for hop in [*middle, late, 1]:
        arrived[hop] = exchange(out, "row", hop)

    plan, total, spread = pl.pallas_call(
        functools.partial(plan_kernel, stages, region, freq_count),
        out_shape=(
            pltpu.SMEM((4 * width,), jnp.int32),
            pltpu.VMEM(image_shape, F32),
            pltpu.VMEM(spread_shape, BF16),
        ),
        in_specs=[SMEM_SPEC] * 5 + [VMEM_SPEC],
        out_specs=(SMEM_SPEC,) + (VMEM_SPEC,) * 2,
        compiler_params=params(),
        cost_estimate=cost(4 * tiles.size),
        name="plan_stage",
    )(table, tile_src, tile_dst, block_owner[:, 0], block_slot, token)

    def near(stage, total):
        sources = [arrived[hop] for hop in stages[stage]]
        scratch = pltpu.VMEM((len(sources) * block_count + 1, rows_twice, node_count), BF16)
        return pl.pallas_call(
            functools.partial(near_kernel, stage, region, len(sources)),
            out_shape=pltpu.VMEM(image_shape, F32),
            in_specs=[SMEM_SPEC] + [VMEM_SPEC] * (len(sources) + 2),
            out_specs=VMEM_SPEC,
            scratch_shapes=[scratch],
            input_output_aliases={len(sources) + 2: 0},
            compiler_params=params(),
            cost_estimate=cost(SMALL),
            name="near_stage",
        )(plan, *sources, tiles, total)

    def forward(hop, total):
        arrived[hop], total = lax.optimization_barrier((arrived[hop], total))
        arrived[hop + 1] = exchange(arrived[hop], "row", 1)
        return total

    total = near(0, total)
    for hop in middle:
        total = forward(hop, total)
    total = near(1, total)
    weights, total = lax.optimization_barrier((areas, total))
    basis = pl.pallas_call(
        basis_kernel,
        out_shape=pltpu.VMEM(basis_shape, F32),
        in_specs=[VMEM_SPEC] * 2,
        out_specs=VMEM_SPEC,
        compiler_params=params(),
        cost_estimate=cost(SMALL),
        name="basis_stage",
    )(jnp.transpose(geometry, (1, 0, 2)), weights)
    total = forward(late, total)
    total = near(2, total)

    total, field, table, powers, crosses = pl.pallas_call(
        functools.partial(field_kernel, 3, region, 1),
        out_shape=(
            pltpu.VMEM(image_shape, F32),
            pltpu.VMEM(panels.shape, F32),
            pltpu.VMEM(table_shape, F32),
            pltpu.VMEM(power_shape, F32),
            pltpu.VMEM(power_shape, F32),
        ),
        in_specs=[SMEM_SPEC] + [VMEM_SPEC] * 6,
        out_specs=(VMEM_SPEC,) * 5,
        scratch_shapes=[pltpu.VMEM((block_count + 1, rows_twice, node_count), BF16)],
        input_output_aliases={4: 0},
        compiler_params=params(),
        cost_estimate=cost(SMALL),
        name="field_stage",
    )(plan, arrived[late + 1], panels, tiles, total, basis, spread)

    tables = [table]
    for distance in range(1, group_count):
        tables.append(exchange(table, "col", distance))

    gradient = pl.pallas_call(
        functools.partial(gradient_kernel, len(tables)),
        out_shape=jax.ShapeDtypeStruct((block_count, node_count), F32),
        in_specs=[VMEM_SPEC] * (len(tables) + 4),
        out_specs=VMEM_SPEC,
        compiler_params=params(),
        cost_estimate=cost(SMALL),
        name="gradient_stage",
    )(*tables, basis, spread, powers, crosses)
    return (field, gradient)


def solution(mesh):
    in_specs = (
        P(("row", "col"), None, None),
        P(("row", "col"), None, None),
        P(("row", "col")),
        P(("row", "col")),
        P(("row", "col"), None, None),
        P(("row", "col"), None),
        P(("row", "col"), None),
        P(("row", "col")),
    )
    out_specs = (P(("row", "col"), None, None), P(("row", "col"), None))
    return jax.shard_map(shards, mesh=mesh, in_specs=in_specs, out_specs=out_specs, check_vma=False)
```

```python
import functools

import jax
import jax.numpy as jnp
from jax import lax
from jax.experimental import pallas as pl
from jax.experimental.pallas import tpu as pltpu
from jax.sharding import PartitionSpec as P

PD = 4
EPSILON = 1e-05
UNROLL = 8
MOMENTS = 8
SMALL = 1 << 16
STAGE_SHIFT = 16
F32 = jnp.float32
BF16 = jnp.bfloat16
VMEM_LIMIT = 8 << 20
EARLY_LIMIT = 44 << 20

VMEM_SPEC = pl.BlockSpec(memory_space=pltpu.VMEM)
SMEM_SPEC = pl.BlockSpec(memory_space=pltpu.SMEM)
HBM_SPEC = pl.BlockSpec(memory_space=pltpu.HBM)


def cost(size):
    return pl.CostEstimate(flops=0, bytes_accessed=size, transcendentals=0)


def params(limit=VMEM_LIMIT):
    return pltpu.CompilerParams(vmem_limit_bytes=limit)


def parts_of(values, count):
    parts = []
    for _ in range(count - 1):
        part = values.astype(BF16)
        parts.append(part)
        values = values - part.astype(F32)
    parts.append(values.astype(BF16))
    return parts


def dot(left, right, transposed=False):
    axes = (((1,), (1 if transposed else 0,)), ((), ()))
    return lax.dot_general(left, right, axes, preferred_element_type=F32)


def dot_near_exact(left, right, transposed=False):
    rows = left.shape[0]
    left_high, left_low = parts_of(left, 2)
    right_high, right_low = parts_of(right, 2)
    both = dot(jnp.concatenate([left_high, left_low], axis=0), right_high, transposed)
    return both[:rows] + (both[rows:] + dot(left_high, right_low, transposed))


def block_mask(block_count, freq_count):
    shape = (block_count, block_count * freq_count)
    rows = lax.broadcasted_iota(jnp.int32, shape, 0)
    columns = lax.broadcasted_iota(jnp.int32, shape, 1)
    return (columns // freq_count == rows).astype(F32)


def fill_panels(sources, held):
    depth = sources[0].shape[0]
    for index, source in enumerate(sources):
        held[index * depth : (index + 1) * depth] = source[...]
    held[len(sources) * depth] = jnp.zeros(held.shape[1:], held.dtype)


def add_stage(stage, region, plan, held, tiles, total):
    width = plan.shape[0] // 4
    count = plan[3 * width + stage]
    whole = count // UNROLL

    def add_group(base, size):
        images = [
            dot(held[plan[width + base + lane]], tiles[plan[base + lane]])
            for lane in range(size)
        ]
        for lane in range(size):
            target = plan[2 * width + base + lane]
            total[target] += images[lane]

    def body(step, carry):
        add_group(stage * region + step * UNROLL, UNROLL)
        return carry

    lax.fori_loop(0, whole, body, 0)
    left = count - whole * UNROLL
    for size in range(2, UNROLL + 1, 2):

        @pl.when((left > size - 2) & (left <= size))
        def _(size=size):
            add_group(stage * region + whole * UNROLL, size)


def early_kernel(tiles, token):
    token[...] = jnp.zeros_like(token)


def plan_kernel(stages, region, freq_count, table, src, dst, owner, slot, token, plan, total, spread):
    block_count = owner.shape[0]
    width = plan.shape[0] // 4
    me = lax.axis_index("row")

    def place_tile(t, counts):
        source = src[t]
        found = table[lax.div(source, block_count) ^ me]
        stage_here = lax.shift_right_logical(found, STAGE_SHIFT)
        target = jnp.int32(0)
        for stage in range(len(stages)):
            target = jnp.where(stage_here == stage, stage * region + counts[stage], target)
        plan[target] = t
        plan[width + target] = (found & (2**STAGE_SHIFT - 1)) + lax.rem(source, block_count)
        plan[2 * width + target] = dst[t]
        return tuple(
            count + (stage_here == stage).astype(jnp.int32) for stage, count in enumerate(counts)
        )

    counts = lax.fori_loop(0, src.shape[0], place_tile, (jnp.int32(0),) * len(stages), unroll=8)
    for stage, held in enumerate(stages):
        plan[3 * width + stage] = counts[stage]
        for lane in range(UNROLL):
            position = stage * region + counts[stage] + lane
            plan[position] = 0
            plan[width + position] = len(held) * block_count
            plan[2 * width + position] = 0
    total[...] = jnp.zeros_like(total)
    shape = (freq_count, spread.shape[1])
    lanes = lax.broadcasted_iota(jnp.int32, shape, 1)
    same = lanes % freq_count == lax.broadcasted_iota(jnp.int32, shape, 0)
    for block in range(block_count):
        particle = owner[block] * PD + slot[block]
        chosen = same & (lanes // freq_count == particle)
        spread[block * freq_count : (block + 1) * freq_count] = jnp.where(
            chosen, 1.0, 0.0
        ).astype(BF16)


def basis_kernel(place, areas, basis):
    block_count = areas.shape[0]
    nx, ny, nz, px, py, pz = [place[i] for i in range(6)]
    weight = areas[...]
    rows = [nx, ny, nz, py * nz - pz * ny, pz * nx - px * nz, px * ny - py * nx]
    for index, row in enumerate(rows):
        basis[index * block_count : (index + 1) * block_count] = weight * row
    for index in range(len(rows), MOMENTS):
        basis[index * block_count : (index + 1) * block_count] = weight


def near_kernel(stage, region, count, plan, *refs):
    sources = refs[:count]
    tiles, start, total, held = refs[count:]
    fill_panels(sources, held)
    add_stage(stage, region, plan, held, tiles, total)


def field_kernel(stage, region, count, plan, *refs):
    sources = refs[:count]
    panels, tiles, start, basis, spread = refs[count : count + 5]
    total, field, table, powers, crosses, held = refs[count + 5 :]
    block_count, rows_twice, node_count = panels.shape
    freq_count = rows_twice // 2
    fill_panels(sources, held)
    add_stage(stage, region, plan, held, tiles, total)
    for block in range(block_count):
        image = total[block]
        incident = panels[block].astype(F32)
        real_in, imag_in = incident[:freq_count], incident[freq_count:]
        real = 0.5 * real_in + (
            image[:freq_count, :node_count] - image[freq_count:, node_count:]
        )
        imag = 0.5 * imag_in + (
            image[:freq_count, node_count:] + image[freq_count:, :node_count]
        )
        field[block, :freq_count] = real
        field[block, freq_count:] = imag
        span = slice(block * freq_count, (block + 1) * freq_count)
        powers[span] = real * real + imag * imag
        crosses[span] = real_in * real + imag_in * imag
    last = (MOMENTS - 1) * block_count
    first_moments = dot_near_exact(basis[:last], powers[...], True)
    last_moment = dot_near_exact(basis[last:], crosses[...], True)
    mask = block_mask(block_count, freq_count)
    pieces = [
        jnp.sum(mask * first_moments[k * block_count : (k + 1) * block_count], axis=0, keepdims=True)
        for k in range(MOMENTS - 1)
    ]
    pieces.append(jnp.sum(mask * last_moment, axis=0, keepdims=True))
    moments = jnp.concatenate(pieces, axis=0)
    joined = dot(jnp.concatenate(parts_of(moments, 3), axis=0), spread[...])
    table[...] = joined[:MOMENTS] + (joined[MOMENTS : 2 * MOMENTS] + joined[2 * MOMENTS :])


def gradient_kernel(count, *refs):
    tables = refs[:count]
    basis, spread, powers, crosses, gradient = refs[count:]
    block_count = gradient.shape[0]
    freq_count = powers.shape[0] // block_count
    summed = tables[0][...]
    for table in tables[1:]:
        summed = summed + table[...]
    joined = dot(jnp.concatenate(parts_of(summed, 3), axis=0), spread[...], True)
    totals = joined[:MOMENTS] + (joined[MOMENTS : 2 * MOMENTS] + joined[2 * MOMENTS :])
    mask = block_mask(block_count, freq_count)
    squares = jnp.sum(totals * totals, axis=0, keepdims=True)
    mean = jnp.sum(mask * squares, axis=1, keepdims=True) / (MOMENTS * freq_count)
    scale = lax.rsqrt(mean + EPSILON) / freq_count
    spots = [mask * totals[k : k + 1] for k in range(MOMENTS)]
    first_terms = dot_near_exact(jnp.concatenate(spots[:-1], axis=0), powers[...])
    last_term = dot_near_exact(spots[-1], crosses[...])
    result = basis[(MOMENTS - 1) * block_count :] * last_term
    for k in range(MOMENTS - 1):
        span = slice(k * block_count, (k + 1) * block_count)
        result = result + basis[span] * first_terms[span]
    gradient[...] = result * scale


def exchange(values, axis, hop):
    pairs = [(i, i ^ hop) for i in range(lax.axis_size(axis))]
    return lax.ppermute(values, axis, pairs)


def shards(panels, tiles, tile_dst, tile_src, geometry, areas, block_owner, block_slot):
    block_count, rows_twice, node_count = panels.shape
    freq_count = rows_twice // 2
    tile_count = tiles.shape[0]
    row_count = lax.axis_size("row")
    group_count = lax.axis_size("col")
    particle_count = group_count * PD
    image_shape = (block_count, rows_twice, 2 * node_count)
    basis_shape = (MOMENTS * block_count, node_count)
    spread_shape = (block_count * freq_count, particle_count * freq_count)
    power_shape = (block_count * freq_count, node_count)
    table_shape = (MOMENTS, particle_count * freq_count)
    region = tile_count + UNROLL

    token = pl.pallas_call(
        early_kernel,
        out_shape=pltpu.VMEM((8, 128), F32),
        in_specs=[HBM_SPEC],
        out_specs=VMEM_SPEC,
        compiler_params=params(EARLY_LIMIT),
        cost_estimate=cost(4 * tiles.size),
        name="early_stage",
    )(tiles)

    first, late = row_count // 2, row_count - 2
    middle = [first, *[hop for hop in range(2, row_count, 2) if hop not in (first, late)]]
    stages = ([0], [*middle, 1], [*[hop + 1 for hop in middle], late], [late + 1])
    places = {
        hop: (stage << STAGE_SHIFT) + index * block_count
        for stage, hops in enumerate(stages)
        for index, hop in enumerate(hops)
    }
    table = jnp.array([places[hop] for hop in range(row_count)], jnp.int32)
    width = -(-(len(stages) * region) // 128) * 128

    arrived = {0: panels}
    token, out = lax.optimization_barrier((token, panels))
    for hop in [*middle, late, 1]:
        arrived[hop] = exchange(out, "row", hop)

    plan, total, spread = pl.pallas_call(
        functools.partial(plan_kernel, stages, region, freq_count),
        out_shape=(
            pltpu.SMEM((4 * width,), jnp.int32),
            pltpu.VMEM(image_shape, F32),
            pltpu.VMEM(spread_shape, BF16),
        ),
        in_specs=[SMEM_SPEC] * 5 + [VMEM_SPEC],
        out_specs=(SMEM_SPEC,) + (VMEM_SPEC,) * 2,
        compiler_params=params(),
        cost_estimate=cost(4 * tiles.size),
        name="plan_stage",
    )(table, tile_src, tile_dst, block_owner[:, 0], block_slot, token)

    def near(stage, total):
        sources = [arrived[hop] for hop in stages[stage]]
        scratch = pltpu.VMEM((len(sources) * block_count + 1, rows_twice, node_count), BF16)
        return pl.pallas_call(
            functools.partial(near_kernel, stage, region, len(sources)),
            out_shape=pltpu.VMEM(image_shape, F32),
            in_specs=[SMEM_SPEC] + [VMEM_SPEC] * (len(sources) + 2),
            out_specs=VMEM_SPEC,
            scratch_shapes=[scratch],
            input_output_aliases={len(sources) + 2: 0},
            compiler_params=params(),
            cost_estimate=cost(SMALL),
            name="near_stage",
        )(plan, *sources, tiles, total)

    def forward(hop, total):
        arrived[hop], total = lax.optimization_barrier((arrived[hop], total))
        arrived[hop + 1] = exchange(arrived[hop], "row", 1)
        return total

    total = near(0, total)
    for hop in middle:
        total = forward(hop, total)
    total = near(1, total)
    weights, total = lax.optimization_barrier((areas, total))
    basis = pl.pallas_call(
        basis_kernel,
        out_shape=pltpu.VMEM(basis_shape, F32),
        in_specs=[VMEM_SPEC] * 2,
        out_specs=VMEM_SPEC,
        compiler_params=params(),
        cost_estimate=cost(SMALL),
        name="basis_stage",
    )(jnp.transpose(geometry, (1, 0, 2)), weights)
    total = forward(late, total)
    total = near(2, total)

    total, field, table, powers, crosses = pl.pallas_call(
        functools.partial(field_kernel, 3, region, 1),
        out_shape=(
            pltpu.VMEM(image_shape, F32),
            pltpu.VMEM(panels.shape, F32),
            pltpu.VMEM(table_shape, F32),
            pltpu.VMEM(power_shape, F32),
            pltpu.VMEM(power_shape, F32),
        ),
        in_specs=[SMEM_SPEC] + [VMEM_SPEC] * 6,
        out_specs=(VMEM_SPEC,) * 5,
        scratch_shapes=[pltpu.VMEM((block_count + 1, rows_twice, node_count), BF16)],
        input_output_aliases={4: 0},
        compiler_params=params(),
        cost_estimate=cost(SMALL),
        name="field_stage",
    )(plan, arrived[late + 1], panels, tiles, total, basis, spread)

    tables = [table]
    for distance in range(1, group_count):
        tables.append(exchange(table, "col", distance))

    gradient = pl.pallas_call(
        functools.partial(gradient_kernel, len(tables)),
        out_shape=jax.ShapeDtypeStruct((block_count, node_count), F32),
        in_specs=[VMEM_SPEC] * (len(tables) + 4),
        out_specs=VMEM_SPEC,
        compiler_params=params(),
        cost_estimate=cost(SMALL),
        name="gradient_stage",
    )(*tables, basis, spread, powers, crosses)
    return (field, gradient)


def solution(mesh):
    in_specs = (
        P(("row", "col"), None, None),
        P(("row", "col"), None, None),
        P(("row", "col")),
        P(("row", "col")),
        P(("row", "col"), None, None),
        P(("row", "col"), None),
        P(("row", "col"), None),
        P(("row", "col")),
    )
    out_specs = (P(("row", "col"), None, None), P(("row", "col"), None))
    return jax.shard_map(shards, mesh=mesh, in_specs=in_specs, out_specs=out_specs, check_vma=False)
```

```python
import functools

import jax
import jax.numpy as jnp
from jax import lax
from jax.experimental import pallas as pl
from jax.experimental.pallas import tpu as pltpu
from jax.sharding import PartitionSpec as P

PD = 4
EPSILON = 1e-05
UNROLL = 8
MOMENTS = 8
SMALL = 1 << 16
STAGE_SHIFT = 16
F32 = jnp.float32
BF16 = jnp.bfloat16
VMEM_LIMIT = 8 << 20
EARLY_LIMIT = 44 << 20

VMEM_SPEC = pl.BlockSpec(memory_space=pltpu.VMEM)
SMEM_SPEC = pl.BlockSpec(memory_space=pltpu.SMEM)
HBM_SPEC = pl.BlockSpec(memory_space=pltpu.HBM)


def cost(size):
    return pl.CostEstimate(flops=0, bytes_accessed=size, transcendentals=0)


def params(limit=VMEM_LIMIT):
    return pltpu.CompilerParams(vmem_limit_bytes=limit)


def parts_of(values, count):
    parts = []
    for _ in range(count - 1):
        part = values.astype(BF16)
        parts.append(part)
        values = values - part.astype(F32)
    parts.append(values.astype(BF16))
    return parts


def dot(left, right, transposed=False):
    axes = (((1,), (1 if transposed else 0,)), ((), ()))
    return lax.dot_general(left, right, axes, preferred_element_type=F32)


def dot_near_exact(left, right, transposed=False):
    rows = left.shape[0]
    left_high, left_low = parts_of(left, 2)
    right_high, right_low = parts_of(right, 2)
    both = dot(jnp.concatenate([left_high, left_low], axis=0), right_high, transposed)
    return both[:rows] + (both[rows:] + dot(left_high, right_low, transposed))


def block_mask(block_count, freq_count):
    shape = (block_count, block_count * freq_count)
    rows = lax.broadcasted_iota(jnp.int32, shape, 0)
    columns = lax.broadcasted_iota(jnp.int32, shape, 1)
    return (columns // freq_count == rows).astype(F32)


def fill_panels(sources, held):
    depth = sources[0].shape[0]
    for index, source in enumerate(sources):
        held[index * depth : (index + 1) * depth] = source[...]


def add_stage(stage, region, plan, held, tiles, total):
    width = plan.shape[0] // 4
    count = plan[3 * width + stage]
    whole = count // UNROLL

    def add_group(base, size):
        images = [
            dot(held[plan[width + base + lane]], tiles[plan[base + lane]])
            for lane in range(size)
        ]
        for lane in range(size):
            target = plan[2 * width + base + lane]
            total[target] += images[lane]

    def body(step, carry):
        add_group(stage * region + step * UNROLL, UNROLL)
        return carry

    lax.fori_loop(0, whole, body, 0)
    left = count - whole * UNROLL
    for size in range(2, UNROLL + 1, 2):

        @pl.when((left > size - 2) & (left <= size))
        def _(size=size):
            add_group(stage * region + whole * UNROLL, size)


def early_kernel(tiles, token):
    token[...] = jnp.zeros_like(token)


def plan_kernel(
    stages, region, freq_count, table, src, dst, owner, slot, token, plan, total, spread, collect
):
    block_count = owner.shape[0]
    width = plan.shape[0] // 4
    me = lax.axis_index("row")

    def place_tile(t, counts):
        source = src[t]
        found = table[lax.div(source, block_count) ^ me]
        stage_here = lax.shift_right_logical(found, STAGE_SHIFT)
        target = jnp.int32(0)
        for stage in range(len(stages)):
            target = jnp.where(stage_here == stage, stage * region + counts[stage], target)
        plan[target] = t
        plan[width + target] = (found & (2**STAGE_SHIFT - 1)) + lax.rem(source, block_count)
        plan[2 * width + target] = dst[t]
        return tuple(
            count + (stage_here == stage).astype(jnp.int32) for stage, count in enumerate(counts)
        )

    counts = lax.fori_loop(0, src.shape[0], place_tile, (jnp.int32(0),) * len(stages), unroll=8)
    for stage in range(len(stages)):
        plan[3 * width + stage] = counts[stage]
        for lane in range(UNROLL):
            position = stage * region + counts[stage] + lane
            plan[position] = 0
            plan[width + position] = 0
            plan[2 * width + position] = block_count
    total[...] = jnp.zeros_like(total)
    shape = (freq_count, spread.shape[1])
    lanes = lax.broadcasted_iota(jnp.int32, shape, 1)
    same = lanes % freq_count == lax.broadcasted_iota(jnp.int32, shape, 0)
    for block in range(block_count):
        particle = owner[block] * PD + slot[block]
        chosen = same & (lanes // freq_count == particle)
        spread[block * freq_count : (block + 1) * freq_count] = jnp.where(
            chosen, 1.0, 0.0
        ).astype(BF16)
    rows = lax.broadcasted_iota(jnp.int32, collect.shape, 0)
    lanes = lax.broadcasted_iota(jnp.int32, collect.shape, 1)
    wanted = lanes % freq_count
    for block in range(block_count):
        particle = owner[block] * PD + slot[block]
        wanted = wanted + jnp.where(lanes // freq_count == block, particle * freq_count, 0)
    collect[...] = jnp.where(rows == wanted, 1.0, 0.0).astype(BF16)


def basis_kernel(place, areas, basis):
    block_count = areas.shape[0]
    nx, ny, nz, px, py, pz = [place[i] for i in range(6)]
    weight = areas[...]
    rows = [nx, ny, nz, py * nz - pz * ny, pz * nx - px * nz, px * ny - py * nx]
    for index, row in enumerate(rows):
        basis[index * block_count : (index + 1) * block_count] = weight * row
    for index in range(len(rows), MOMENTS):
        basis[index * block_count : (index + 1) * block_count] = weight


def near_kernel(stage, region, count, plan, *refs):
    sources = refs[:count]
    tiles, start, total, *held = refs[count:]
    if held:
        fill_panels(sources, held[0])
    add_stage(stage, region, plan, held[0] if held else sources[0], tiles, total)


def field_kernel(
    stage, region, plan, source, panels, tiles, start, basis, spread,
    total, field, table, powers, crosses,
):
    block_count, rows_twice, node_count = panels.shape
    freq_count = rows_twice // 2
    add_stage(stage, region, plan, source, tiles, total)
    for block in range(block_count):
        image = total[block]
        incident = panels[block].astype(F32)
        real_in, imag_in = incident[:freq_count], incident[freq_count:]
        real = 0.5 * real_in + (
            image[:freq_count, :node_count] - image[freq_count:, node_count:]
        )
        imag = 0.5 * imag_in + (
            image[:freq_count, node_count:] + image[freq_count:, :node_count]
        )
        field[block, :freq_count] = real
        field[block, freq_count:] = imag
        span = slice(block * freq_count, (block + 1) * freq_count)
        powers[span] = real * real + imag * imag
        crosses[span] = real_in * real + imag_in * imag
    last = (MOMENTS - 1) * block_count
    first_moments = dot_near_exact(basis[:last], powers[...], True)
    last_moment = dot_near_exact(basis[last:], crosses[...], True)
    mask = block_mask(block_count, freq_count)
    pieces = [
        jnp.sum(mask * first_moments[k * block_count : (k + 1) * block_count], axis=0, keepdims=True)
        for k in range(MOMENTS - 1)
    ]
    pieces.append(jnp.sum(mask * last_moment, axis=0, keepdims=True))
    moments = jnp.concatenate(pieces, axis=0)
    joined = dot(jnp.concatenate(parts_of(moments, 3), axis=0), spread[...])
    table[...] = joined[:MOMENTS] + (joined[MOMENTS : 2 * MOMENTS] + joined[2 * MOMENTS :])


def gradient_kernel(count, *refs):
    tables = refs[:count]
    basis, collect, powers, crosses, gradient = refs[count:]
    block_count = gradient.shape[0]
    freq_count = powers.shape[0] // block_count
    summed = tables[0][...]
    for table in tables[1:]:
        summed = summed + table[...]
    joined = dot(jnp.concatenate(parts_of(summed, 3), axis=0), collect[...])
    totals = joined[:MOMENTS] + (joined[MOMENTS : 2 * MOMENTS] + joined[2 * MOMENTS :])
    mask = block_mask(block_count, freq_count)
    squares = jnp.sum(totals * totals, axis=0, keepdims=True)
    mean = jnp.sum(mask * squares, axis=1, keepdims=True) / (MOMENTS * freq_count)
    scale = lax.rsqrt(mean + EPSILON) / freq_count
    spots = [mask * totals[k : k + 1] for k in range(MOMENTS)]
    first_terms = dot_near_exact(jnp.concatenate(spots[:-1], axis=0), powers[...])
    last_term = dot_near_exact(spots[-1], crosses[...])
    result = basis[(MOMENTS - 1) * block_count :] * last_term
    for k in range(MOMENTS - 1):
        span = slice(k * block_count, (k + 1) * block_count)
        result = result + basis[span] * first_terms[span]
    gradient[...] = result * scale


def exchange(values, axis, hop):
    pairs = [(i, i ^ hop) for i in range(lax.axis_size(axis))]
    return lax.ppermute(values, axis, pairs)


def shards(panels, tiles, tile_dst, tile_src, geometry, areas, block_owner, block_slot):
    block_count, rows_twice, node_count = panels.shape
    freq_count = rows_twice // 2
    tile_count = tiles.shape[0]
    row_count = lax.axis_size("row")
    group_count = lax.axis_size("col")
    particle_count = group_count * PD
    image_shape = (block_count + 1, rows_twice, 2 * node_count)
    basis_shape = (MOMENTS * block_count, node_count)
    spread_shape = (block_count * freq_count, particle_count * freq_count)
    power_shape = (block_count * freq_count, node_count)
    table_shape = (MOMENTS, particle_count * freq_count)
    region = tile_count + UNROLL

    token = pl.pallas_call(
        early_kernel,
        out_shape=pltpu.VMEM((8, 128), F32),
        in_specs=[HBM_SPEC],
        out_specs=VMEM_SPEC,
        compiler_params=params(EARLY_LIMIT),
        cost_estimate=cost(4 * tiles.size),
        name="early_stage",
    )(tiles)

    first, late = row_count // 2, row_count - 2
    middle = [first, *[hop for hop in range(2, row_count, 2) if hop not in (first, late)]]
    stages = ([0], [*middle, 1], [*[hop + 1 for hop in middle], late], [late + 1])
    places = {
        hop: (stage << STAGE_SHIFT) + index * block_count
        for stage, hops in enumerate(stages)
        for index, hop in enumerate(hops)
    }
    table = jnp.array([places[hop] for hop in range(row_count)], jnp.int32)
    width = -(-(len(stages) * region) // 128) * 128

    arrived = {0: panels}
    token, out = lax.optimization_barrier((token, panels))
    for hop in [*middle, late, 1]:
        arrived[hop] = exchange(out, "row", hop)

    plan, total, spread, collect = pl.pallas_call(
        functools.partial(plan_kernel, stages, region, freq_count),
        out_shape=(
            pltpu.SMEM((4 * width,), jnp.int32),
            pltpu.VMEM(image_shape, F32),
            pltpu.VMEM(spread_shape, BF16),
            pltpu.VMEM(spread_shape[::-1], BF16),
        ),
        in_specs=[SMEM_SPEC] * 5 + [VMEM_SPEC],
        out_specs=(SMEM_SPEC,) + (VMEM_SPEC,) * 3,
        compiler_params=params(),
        cost_estimate=cost(4 * tiles.size),
        name="plan_stage",
    )(table, tile_src, tile_dst, block_owner[:, 0], block_slot, token)

    def near(stage, total):
        sources = [arrived[hop] for hop in stages[stage]]
        stacked = pltpu.VMEM((len(sources) * block_count, rows_twice, node_count), BF16)
        return pl.pallas_call(
            functools.partial(near_kernel, stage, region, len(sources)),
            out_shape=pltpu.VMEM(image_shape, F32),
            in_specs=[SMEM_SPEC] + [VMEM_SPEC] * (len(sources) + 2),
            out_specs=VMEM_SPEC,
            scratch_shapes=[stacked] if len(sources) > 1 else [],
            input_output_aliases={len(sources) + 2: 0},
            compiler_params=params(),
            cost_estimate=cost(SMALL),
            name="near_stage",
        )(plan, *sources, tiles, total)

    def forward(hop, total):
        arrived[hop], total = lax.optimization_barrier((arrived[hop], total))
        arrived[hop + 1] = exchange(arrived[hop], "row", 1)
        return total

    total = near(0, total)
    for hop in middle:
        total = forward(hop, total)
    total = near(1, total)
    weights, total = lax.optimization_barrier((areas, total))
    basis = pl.pallas_call(
        basis_kernel,
        out_shape=pltpu.VMEM(basis_shape, F32),
        in_specs=[VMEM_SPEC] * 2,
        out_specs=VMEM_SPEC,
        compiler_params=params(),
        cost_estimate=cost(SMALL),
        name="basis_stage",
    )(jnp.transpose(geometry, (1, 0, 2)), weights)
    total = forward(late, total)
    total = near(2, total)

    total, field, table, powers, crosses = pl.pallas_call(
        functools.partial(field_kernel, 3, region),
        out_shape=(
            pltpu.VMEM(image_shape, F32),
            pltpu.VMEM(panels.shape, F32),
            pltpu.VMEM(table_shape, F32),
            pltpu.VMEM(power_shape, F32),
            pltpu.VMEM(power_shape, F32),
        ),
        in_specs=[SMEM_SPEC] + [VMEM_SPEC] * 6,
        out_specs=(VMEM_SPEC,) * 5,
        input_output_aliases={4: 0},
        compiler_params=params(),
        cost_estimate=cost(SMALL),
        name="field_stage",
    )(plan, arrived[late + 1], panels, tiles, total, basis, spread)

    tables = [table]
    for distance in range(1, group_count):
        tables.append(exchange(table, "col", distance))

    gradient = pl.pallas_call(
        functools.partial(gradient_kernel, len(tables)),
        out_shape=jax.ShapeDtypeStruct((block_count, node_count), F32),
        in_specs=[VMEM_SPEC] * (len(tables) + 4),
        out_specs=VMEM_SPEC,
        compiler_params=params(),
        cost_estimate=cost(SMALL),
        name="gradient_stage",
    )(*tables, basis, collect, powers, crosses)
    return (field, gradient)


def solution(mesh):
    in_specs = (
        P(("row", "col"), None, None),
        P(("row", "col"), None, None),
        P(("row", "col")),
        P(("row", "col")),
        P(("row", "col"), None, None),
        P(("row", "col"), None),
        P(("row", "col"), None),
        P(("row", "col")),
    )
    out_specs = (P(("row", "col"), None, None), P(("row", "col"), None))
    return jax.shard_map(shards, mesh=mesh, in_specs=in_specs, out_specs=out_specs, check_vma=False)
```

```python
import functools

import jax
import jax.numpy as jnp
from jax import lax
from jax.experimental import pallas as pl
from jax.experimental.pallas import tpu as pltpu
from jax.sharding import PartitionSpec as P

PD = 4
EPSILON = 1e-05
UNROLL = 8
MOMENTS = 8
SMALL = 1 << 16
STAGE_SHIFT = 16
F32 = jnp.float32
BF16 = jnp.bfloat16
VMEM_LIMIT = 8 << 20
EARLY_LIMIT = 44 << 20

VMEM_SPEC = pl.BlockSpec(memory_space=pltpu.VMEM)
SMEM_SPEC = pl.BlockSpec(memory_space=pltpu.SMEM)
HBM_SPEC = pl.BlockSpec(memory_space=pltpu.HBM)


def cost(size):
    return pl.CostEstimate(flops=0, bytes_accessed=size, transcendentals=0)


def params(limit=VMEM_LIMIT):
    return pltpu.CompilerParams(vmem_limit_bytes=limit)


def parts_of(values, count):
    parts = []
    for _ in range(count - 1):
        part = values.astype(BF16)
        parts.append(part)
        values = values - part.astype(F32)
    parts.append(values.astype(BF16))
    return parts


def dot(left, right, transposed=False):
    axes = (((1,), (1 if transposed else 0,)), ((), ()))
    return lax.dot_general(left, right, axes, preferred_element_type=F32)


def dot_near_exact(left, right, transposed=False):
    rows = left.shape[0]
    left_high, left_low = parts_of(left, 2)
    right_high, right_low = parts_of(right, 2)
    both = dot(jnp.concatenate([left_high, left_low], axis=0), right_high, transposed)
    return both[:rows] + (both[rows:] + dot(left_high, right_low, transposed))


def block_mask(block_count, freq_count):
    shape = (block_count, block_count * freq_count)
    rows = lax.broadcasted_iota(jnp.int32, shape, 0)
    columns = lax.broadcasted_iota(jnp.int32, shape, 1)
    return (columns // freq_count == rows).astype(F32)


def fill_panels(sources, held):
    depth = sources[0].shape[0]
    for index, source in enumerate(sources):
        held[index * depth : (index + 1) * depth] = source[...]


def add_stage(stage, region, plan, held, tiles, total):
    width = plan.shape[0] // 4
    count = plan[3 * width + stage]
    whole = count // UNROLL

    def add_group(base, size):
        images = [
            dot(held[plan[width + base + lane]], tiles[plan[base + lane]])
            for lane in range(size)
        ]
        for lane in range(size):
            target = plan[2 * width + base + lane]
            total[target] += images[lane]

    def body(step, carry):
        add_group(stage * region + step * UNROLL, UNROLL)
        return carry

    lax.fori_loop(0, whole, body, 0)
    left = count - whole * UNROLL
    for size in range(2, UNROLL + 1, 2):

        @pl.when((left > size - 2) & (left <= size))
        def _(size=size):
            add_group(stage * region + whole * UNROLL, size)


def early_kernel(tiles, token):
    token[...] = jnp.zeros_like(token)


def plan_kernel(
    stages, region, freq_count, table, src, dst, owner, slot, token, plan, total, spread, collect
):
    block_count = owner.shape[0]
    width = plan.shape[0] // 4
    me = lax.axis_index("row")

    def place_tile(t, counts):
        source = src[t]
        found = table[lax.div(source, block_count) ^ me]
        stage_here = lax.shift_right_logical(found, STAGE_SHIFT)
        target = jnp.int32(0)
        for stage in range(len(stages)):
            target = jnp.where(stage_here == stage, stage * region + counts[stage], target)
        plan[target] = t
        plan[width + target] = (found & (2**STAGE_SHIFT - 1)) + lax.rem(source, block_count)
        plan[2 * width + target] = dst[t]
        return tuple(
            count + (stage_here == stage).astype(jnp.int32) for stage, count in enumerate(counts)
        )

    counts = lax.fori_loop(0, src.shape[0], place_tile, (jnp.int32(0),) * len(stages), unroll=8)
    for stage in range(len(stages)):
        plan[3 * width + stage] = counts[stage]
        for lane in range(UNROLL):
            position = stage * region + counts[stage] + lane
            plan[position] = 0
            plan[width + position] = 0
            plan[2 * width + position] = block_count
    total[...] = jnp.zeros_like(total)
    shape = (freq_count, spread.shape[1])
    lanes = lax.broadcasted_iota(jnp.int32, shape, 1)
    same = lanes % freq_count == lax.broadcasted_iota(jnp.int32, shape, 0)
    for block in range(block_count):
        particle = owner[block] * PD + slot[block]
        chosen = same & (lanes // freq_count == particle)
        spread[block * freq_count : (block + 1) * freq_count] = jnp.where(
            chosen, 1.0, 0.0
        ).astype(BF16)
    rows = lax.broadcasted_iota(jnp.int32, collect.shape, 0)
    lanes = lax.broadcasted_iota(jnp.int32, collect.shape, 1)
    wanted = lanes % freq_count
    for block in range(block_count):
        particle = owner[block] * PD + slot[block]
        wanted = wanted + jnp.where(lanes // freq_count == block, particle * freq_count, 0)
    collect[...] = jnp.where(rows == wanted, 1.0, 0.0).astype(BF16)


def basis_kernel(place, areas, basis):
    block_count = areas.shape[0]
    nx, ny, nz, px, py, pz = [place[i] for i in range(6)]
    weight = areas[...]
    rows = [nx, ny, nz, py * nz - pz * ny, pz * nx - px * nz, px * ny - py * nx]
    for index, row in enumerate(rows):
        basis[index * block_count : (index + 1) * block_count] = weight * row
    for index in range(len(rows), MOMENTS):
        basis[index * block_count : (index + 1) * block_count] = weight


def near_kernel(stage, region, count, plan, *refs):
    sources = refs[:count]
    tiles, start, total, *held = refs[count:]
    total[...] = start[...]
    if held:
        fill_panels(sources, held[0])
    add_stage(stage, region, plan, held[0] if held else sources[0], tiles, total)


def field_kernel(
    stage, region, plan, source, panels, tiles, start, basis, spread,
    field, table, powers, crosses, total,
):
    block_count, rows_twice, node_count = panels.shape
    freq_count = rows_twice // 2
    total[...] = start[...]
    add_stage(stage, region, plan, source, tiles, total)
    for block in range(block_count):
        image = total[block]
        incident = panels[block].astype(F32)
        real_in, imag_in = incident[:freq_count], incident[freq_count:]
        real = 0.5 * real_in + (
            image[:freq_count, :node_count] - image[freq_count:, node_count:]
        )
        imag = 0.5 * imag_in + (
            image[:freq_count, node_count:] + image[freq_count:, :node_count]
        )
        field[block, :freq_count] = real
        field[block, freq_count:] = imag
        span = slice(block * freq_count, (block + 1) * freq_count)
        powers[span] = real * real + imag * imag
        crosses[span] = real_in * real + imag_in * imag
    last = (MOMENTS - 1) * block_count
    first_moments = dot_near_exact(basis[:last], powers[...], True)
    last_moment = dot_near_exact(basis[last:], crosses[...], True)
    mask = block_mask(block_count, freq_count)
    pieces = [
        jnp.sum(mask * first_moments[k * block_count : (k + 1) * block_count], axis=0, keepdims=True)
        for k in range(MOMENTS - 1)
    ]
    pieces.append(jnp.sum(mask * last_moment, axis=0, keepdims=True))
    moments = jnp.concatenate(pieces, axis=0)
    joined = dot(jnp.concatenate(parts_of(moments, 3), axis=0), spread[...])
    table[...] = joined[:MOMENTS] + (joined[MOMENTS : 2 * MOMENTS] + joined[2 * MOMENTS :])


def gradient_kernel(count, *refs):
    tables = refs[:count]
    basis, collect, powers, crosses, gradient = refs[count:]
    block_count = gradient.shape[0]
    freq_count = powers.shape[0] // block_count
    summed = tables[0][...]
    for table in tables[1:]:
        summed = summed + table[...]
    joined = dot(jnp.concatenate(parts_of(summed, 3), axis=0), collect[...])
    totals = joined[:MOMENTS] + (joined[MOMENTS : 2 * MOMENTS] + joined[2 * MOMENTS :])
    mask = block_mask(block_count, freq_count)
    squares = jnp.sum(totals * totals, axis=0, keepdims=True)
    mean = jnp.sum(mask * squares, axis=1, keepdims=True) / (MOMENTS * freq_count)
    scale = lax.rsqrt(mean + EPSILON) / freq_count
    spots = [mask * totals[k : k + 1] for k in range(MOMENTS)]
    first_terms = dot_near_exact(jnp.concatenate(spots[:-1], axis=0), powers[...])
    last_term = dot_near_exact(spots[-1], crosses[...])
    result = basis[(MOMENTS - 1) * block_count :] * last_term
    for k in range(MOMENTS - 1):
        span = slice(k * block_count, (k + 1) * block_count)
        result = result + basis[span] * first_terms[span]
    gradient[...] = result * scale


def exchange(values, axis, hop):
    pairs = [(i, i ^ hop) for i in range(lax.axis_size(axis))]
    return lax.ppermute(values, axis, pairs)


def shards(panels, tiles, tile_dst, tile_src, geometry, areas, block_owner, block_slot):
    block_count, rows_twice, node_count = panels.shape
    freq_count = rows_twice // 2
    tile_count = tiles.shape[0]
    row_count = lax.axis_size("row")
    group_count = lax.axis_size("col")
    particle_count = group_count * PD
    image_shape = (block_count + 1, rows_twice, 2 * node_count)
    basis_shape = (MOMENTS * block_count, node_count)
    spread_shape = (block_count * freq_count, particle_count * freq_count)
    power_shape = (block_count * freq_count, node_count)
    table_shape = (MOMENTS, particle_count * freq_count)
    region = tile_count + UNROLL

    token = pl.pallas_call(
        early_kernel,
        out_shape=pltpu.VMEM((8, 128), F32),
        in_specs=[HBM_SPEC],
        out_specs=VMEM_SPEC,
        compiler_params=params(EARLY_LIMIT),
        cost_estimate=cost(4 * tiles.size),
        name="early_stage",
    )(tiles)

    first, late = row_count // 2, row_count - 2
    middle = [first, *[hop for hop in range(2, row_count, 2) if hop not in (first, late)]]
    stages = ([0], [*middle, 1], [*[hop + 1 for hop in middle], late], [late + 1])
    places = {
        hop: (stage << STAGE_SHIFT) + index * block_count
        for stage, hops in enumerate(stages)
        for index, hop in enumerate(hops)
    }
    table = jnp.array([places[hop] for hop in range(row_count)], jnp.int32)
    width = -(-(len(stages) * region) // 128) * 128

    arrived = {0: panels}
    token, out = lax.optimization_barrier((token, panels))
    for hop in [*middle, late, 1]:
        arrived[hop] = exchange(out, "row", hop)

    plan, total, spread, collect = pl.pallas_call(
        functools.partial(plan_kernel, stages, region, freq_count),
        out_shape=(
            pltpu.SMEM((4 * width,), jnp.int32),
            pltpu.VMEM(image_shape, F32),
            pltpu.VMEM(spread_shape, BF16),
            pltpu.VMEM(spread_shape[::-1], BF16),
        ),
        in_specs=[SMEM_SPEC] * 5 + [VMEM_SPEC],
        out_specs=(SMEM_SPEC,) + (VMEM_SPEC,) * 3,
        compiler_params=params(),
        cost_estimate=cost(4 * tiles.size),
        name="plan_stage",
    )(table, tile_src, tile_dst, block_owner[:, 0], block_slot, token)

    def near(stage, total):
        sources = [arrived[hop] for hop in stages[stage]]
        stacked = pltpu.VMEM((len(sources) * block_count, rows_twice, node_count), BF16)
        return pl.pallas_call(
            functools.partial(near_kernel, stage, region, len(sources)),
            out_shape=pltpu.VMEM(image_shape, F32),
            in_specs=[SMEM_SPEC] + [VMEM_SPEC] * (len(sources) + 2),
            out_specs=VMEM_SPEC,
            scratch_shapes=[stacked] if len(sources) > 1 else [],
            compiler_params=params(),
            cost_estimate=cost(SMALL),
            name="near_stage",
        )(plan, *sources, tiles, total)

    def forward(hop, total):
        arrived[hop], total = lax.optimization_barrier((arrived[hop], total))
        arrived[hop + 1] = exchange(arrived[hop], "row", 1)
        return total

    total = near(0, total)
    for hop in middle:
        total = forward(hop, total)
    total = near(1, total)
    weights, total = lax.optimization_barrier((areas, total))
    basis = pl.pallas_call(
        basis_kernel,
        out_shape=pltpu.VMEM(basis_shape, F32),
        in_specs=[VMEM_SPEC] * 2,
        out_specs=VMEM_SPEC,
        compiler_params=params(),
        cost_estimate=cost(SMALL),
        name="basis_stage",
    )(jnp.transpose(geometry, (1, 0, 2)), weights)
    total = forward(late, total)
    total = near(2, total)

    field, table, powers, crosses = pl.pallas_call(
        functools.partial(field_kernel, 3, region),
        out_shape=(
            pltpu.VMEM(panels.shape, F32),
            pltpu.VMEM(table_shape, F32),
            pltpu.VMEM(power_shape, F32),
            pltpu.VMEM(power_shape, F32),
        ),
        in_specs=[SMEM_SPEC] + [VMEM_SPEC] * 6,
        out_specs=(VMEM_SPEC,) * 4,
        scratch_shapes=[pltpu.VMEM(image_shape, F32)],
        compiler_params=params(),
        cost_estimate=cost(SMALL),
        name="field_stage",
    )(plan, arrived[late + 1], panels, tiles, total, basis, spread)

    tables = [table]
    for distance in range(group_count - 1, 0, -1):
        tables.append(exchange(table, "col", distance))

    gradient = pl.pallas_call(
        functools.partial(gradient_kernel, len(tables)),
        out_shape=jax.ShapeDtypeStruct((block_count, node_count), F32),
        in_specs=[VMEM_SPEC] * (len(tables) + 4),
        out_specs=VMEM_SPEC,
        compiler_params=params(),
        cost_estimate=cost(SMALL),
        name="gradient_stage",
    )(*tables, basis, collect, powers, crosses)
    return (field, gradient)


def solution(mesh):
    in_specs = (
        P(("row", "col"), None, None),
        P(("row", "col"), None, None),
        P(("row", "col")),
        P(("row", "col")),
        P(("row", "col"), None, None),
        P(("row", "col"), None),
        P(("row", "col"), None),
        P(("row", "col")),
    )
    out_specs = (P(("row", "col"), None, None), P(("row", "col"), None))
    return jax.shard_map(shards, mesh=mesh, in_specs=in_specs, out_specs=out_specs, check_vma=False)
```

```python
import functools

import jax
import jax.numpy as jnp
from jax import lax
from jax.experimental import pallas as pl
from jax.experimental.pallas import tpu as pltpu
from jax.sharding import PartitionSpec as P

PD = 4
EPSILON = 1e-05
UNROLL = 16
MOMENTS = 8
SMALL = 1 << 16
STAGE_SHIFT = 16
F32 = jnp.float32
BF16 = jnp.bfloat16
VMEM_LIMIT = 8 << 20
EARLY_LIMIT = 44 << 20

VMEM_SPEC = pl.BlockSpec(memory_space=pltpu.VMEM)
SMEM_SPEC = pl.BlockSpec(memory_space=pltpu.SMEM)
HBM_SPEC = pl.BlockSpec(memory_space=pltpu.HBM)


def cost(size):
    return pl.CostEstimate(flops=0, bytes_accessed=size, transcendentals=0)


def params(limit=VMEM_LIMIT):
    return pltpu.CompilerParams(vmem_limit_bytes=limit)


def parts_of(values, count):
    parts = []
    for _ in range(count - 1):
        part = values.astype(BF16)
        parts.append(part)
        values = values - part.astype(F32)
    parts.append(values.astype(BF16))
    return parts


def dot(left, right, transposed=False):
    axes = (((1,), (1 if transposed else 0,)), ((), ()))
    return lax.dot_general(left, right, axes, preferred_element_type=F32)


def dot_near_exact(left, right, transposed=False):
    rows = left.shape[0]
    left_high, left_low = parts_of(left, 2)
    right_high, right_low = parts_of(right, 2)
    both = dot(jnp.concatenate([left_high, left_low], axis=0), right_high, transposed)
    return both[:rows] + (both[rows:] + dot(left_high, right_low, transposed))


def block_mask(block_count, freq_count):
    shape = (block_count, block_count * freq_count)
    rows = lax.broadcasted_iota(jnp.int32, shape, 0)
    columns = lax.broadcasted_iota(jnp.int32, shape, 1)
    return (columns // freq_count == rows).astype(F32)


def fill_panels(sources, held):
    depth = sources[0].shape[0]
    for index, source in enumerate(sources):
        held[index * depth : (index + 1) * depth] = source[...]


def add_stage(stage, region, plan, held, tiles, total):
    width = plan.shape[0] // 4
    count = plan[3 * width + stage]
    whole = count // UNROLL

    def add_group(base, size):
        images = [
            dot(held[plan[width + base + lane]], tiles[plan[base + lane]])
            for lane in range(size)
        ]
        for lane in range(size):
            target = plan[2 * width + base + lane]
            total[target] += images[lane]

    def body(step, carry):
        add_group(stage * region + step * UNROLL, UNROLL)
        return carry

    lax.fori_loop(0, whole, body, 0)
    left = count - whole * UNROLL
    for size in range(2, UNROLL + 1, 2):

        @pl.when((left > size - 2) & (left <= size))
        def _(size=size):
            add_group(stage * region + whole * UNROLL, size)


def early_kernel(tiles, token):
    token[...] = jnp.zeros_like(token)


def plan_kernel(
    stages, region, freq_count, table, src, dst, owner, slot, token, plan, total, spread, collect
):
    block_count = owner.shape[0]
    width = plan.shape[0] // 4
    me = lax.axis_index("row")

    def place_tile(t, counts):
        source = src[t]
        found = table[lax.div(source, block_count) ^ me]
        stage_here = lax.shift_right_logical(found, STAGE_SHIFT)
        target = jnp.int32(0)
        for stage in range(len(stages)):
            target = jnp.where(stage_here == stage, stage * region + counts[stage], target)
        plan[target] = t
        plan[width + target] = (found & (2**STAGE_SHIFT - 1)) + lax.rem(source, block_count)
        plan[2 * width + target] = dst[t]
        return tuple(
            count + (stage_here == stage).astype(jnp.int32) for stage, count in enumerate(counts)
        )

    counts = lax.fori_loop(0, src.shape[0], place_tile, (jnp.int32(0),) * len(stages), unroll=8)
    for stage in range(len(stages)):
        plan[3 * width + stage] = counts[stage]
        for lane in range(UNROLL):
            position = stage * region + counts[stage] + lane
            plan[position] = 0
            plan[width + position] = 0
            plan[2 * width + position] = block_count
    total[...] = jnp.zeros_like(total)
    shape = (freq_count, spread.shape[1])
    lanes = lax.broadcasted_iota(jnp.int32, shape, 1)
    same = lanes % freq_count == lax.broadcasted_iota(jnp.int32, shape, 0)
    for block in range(block_count):
        particle = owner[block] * PD + slot[block]
        chosen = same & (lanes // freq_count == particle)
        spread[block * freq_count : (block + 1) * freq_count] = jnp.where(
            chosen, 1.0, 0.0
        ).astype(BF16)
    rows = lax.broadcasted_iota(jnp.int32, collect.shape, 0)
    lanes = lax.broadcasted_iota(jnp.int32, collect.shape, 1)
    wanted = lanes % freq_count
    for block in range(block_count):
        particle = owner[block] * PD + slot[block]
        wanted = wanted + jnp.where(lanes // freq_count == block, particle * freq_count, 0)
    collect[...] = jnp.where(rows == wanted, 1.0, 0.0).astype(BF16)


def basis_kernel(place, areas, basis):
    block_count = areas.shape[0]
    nx, ny, nz, px, py, pz = [place[i] for i in range(6)]
    weight = areas[...]
    rows = [nx, ny, nz, py * nz - pz * ny, pz * nx - px * nz, px * ny - py * nx]
    for index, row in enumerate(rows):
        basis[index * block_count : (index + 1) * block_count] = weight * row
    for index in range(len(rows), MOMENTS):
        basis[index * block_count : (index + 1) * block_count] = weight


def near_kernel(stage, region, count, plan, *refs):
    sources = refs[:count]
    tiles, start, total, *held = refs[count:]
    total[...] = start[...]
    if held:
        fill_panels(sources, held[0])
    add_stage(stage, region, plan, held[0] if held else sources[0], tiles, total)


def field_kernel(
    stage, region, plan, source, panels, tiles, start, basis, spread,
    field, table, powers, crosses, total,
):
    block_count, rows_twice, node_count = panels.shape
    freq_count = rows_twice // 2
    total[...] = start[...]
    add_stage(stage, region, plan, source, tiles, total)
    for block in range(block_count):
        image = total[block]
        incident = panels[block].astype(F32)
        real_in, imag_in = incident[:freq_count], incident[freq_count:]
        real = 0.5 * real_in + (
            image[:freq_count, :node_count] - image[freq_count:, node_count:]
        )
        imag = 0.5 * imag_in + (
            image[:freq_count, node_count:] + image[freq_count:, :node_count]
        )
        field[block, :freq_count] = real
        field[block, freq_count:] = imag
        span = slice(block * freq_count, (block + 1) * freq_count)
        powers[span] = real * real + imag * imag
        crosses[span] = real_in * real + imag_in * imag
    last = (MOMENTS - 1) * block_count
    first_moments = dot_near_exact(basis[:last], powers[...], True)
    last_moment = dot_near_exact(basis[last:], crosses[...], True)
    mask = block_mask(block_count, freq_count)
    pieces = [
        jnp.sum(mask * first_moments[k * block_count : (k + 1) * block_count], axis=0, keepdims=True)
        for k in range(MOMENTS - 1)
    ]
    pieces.append(jnp.sum(mask * last_moment, axis=0, keepdims=True))
    moments = jnp.concatenate(pieces, axis=0)
    joined = dot(jnp.concatenate(parts_of(moments, 3), axis=0), spread[...])
    table[...] = joined[:MOMENTS] + (joined[MOMENTS : 2 * MOMENTS] + joined[2 * MOMENTS :])


def gradient_kernel(count, *refs):
    tables = refs[:count]
    basis, collect, powers, crosses, gradient = refs[count:]
    block_count = gradient.shape[0]
    freq_count = powers.shape[0] // block_count
    summed = tables[0][...]
    for table in tables[1:]:
        summed = summed + table[...]
    joined = dot(jnp.concatenate(parts_of(summed, 3), axis=0), collect[...])
    totals = joined[:MOMENTS] + (joined[MOMENTS : 2 * MOMENTS] + joined[2 * MOMENTS :])
    mask = block_mask(block_count, freq_count)
    squares = jnp.sum(totals * totals, axis=0, keepdims=True)
    mean = jnp.sum(mask * squares, axis=1, keepdims=True) / (MOMENTS * freq_count)
    scale = lax.rsqrt(mean + EPSILON) / freq_count
    spots = [mask * totals[k : k + 1] for k in range(MOMENTS)]
    first_terms = dot_near_exact(jnp.concatenate(spots[:-1], axis=0), powers[...])
    last_term = dot_near_exact(spots[-1], crosses[...])
    result = basis[(MOMENTS - 1) * block_count :] * last_term
    for k in range(MOMENTS - 1):
        span = slice(k * block_count, (k + 1) * block_count)
        result = result + basis[span] * first_terms[span]
    gradient[...] = result * scale


def exchange(values, axis, hop):
    pairs = [(i, i ^ hop) for i in range(lax.axis_size(axis))]
    return lax.ppermute(values, axis, pairs)


def shards(panels, tiles, tile_dst, tile_src, geometry, areas, block_owner, block_slot):
    block_count, rows_twice, node_count = panels.shape
    freq_count = rows_twice // 2
    tile_count = tiles.shape[0]
    row_count = lax.axis_size("row")
    group_count = lax.axis_size("col")
    particle_count = group_count * PD
    image_shape = (block_count + 1, rows_twice, 2 * node_count)
    basis_shape = (MOMENTS * block_count, node_count)
    spread_shape = (block_count * freq_count, particle_count * freq_count)
    power_shape = (block_count * freq_count, node_count)
    table_shape = (MOMENTS, particle_count * freq_count)
    region = tile_count + UNROLL

    token = pl.pallas_call(
        early_kernel,
        out_shape=pltpu.VMEM((8, 128), F32),
        in_specs=[HBM_SPEC],
        out_specs=VMEM_SPEC,
        compiler_params=params(EARLY_LIMIT),
        cost_estimate=cost(4 * tiles.size),
        name="early_stage",
    )(tiles)

    first, late = row_count // 2, row_count - 2
    middle = [first, *[hop for hop in range(2, row_count, 2) if hop not in (first, late)]]
    stages = ([0], [*middle, 1], [*[hop + 1 for hop in middle], late], [late + 1])
    places = {
        hop: (stage << STAGE_SHIFT) + index * block_count
        for stage, hops in enumerate(stages)
        for index, hop in enumerate(hops)
    }
    table = jnp.array([places[hop] for hop in range(row_count)], jnp.int32)
    width = -(-(len(stages) * region) // 128) * 128

    arrived = {0: panels}
    token, out = lax.optimization_barrier((token, panels))
    for hop in [*middle, late, 1]:
        arrived[hop] = exchange(out, "row", hop)

    plan, total, spread, collect = pl.pallas_call(
        functools.partial(plan_kernel, stages, region, freq_count),
        out_shape=(
            pltpu.SMEM((4 * width,), jnp.int32),
            pltpu.VMEM(image_shape, F32),
            pltpu.VMEM(spread_shape, BF16),
            pltpu.VMEM(spread_shape[::-1], BF16),
        ),
        in_specs=[SMEM_SPEC] * 5 + [VMEM_SPEC],
        out_specs=(SMEM_SPEC,) + (VMEM_SPEC,) * 3,
        compiler_params=params(),
        cost_estimate=cost(4 * tiles.size),
        name="plan_stage",
    )(table, tile_src, tile_dst, block_owner[:, 0], block_slot, token)

    def near(stage, total):
        sources = [arrived[hop] for hop in stages[stage]]
        stacked = pltpu.VMEM((len(sources) * block_count, rows_twice, node_count), BF16)
        return pl.pallas_call(
            functools.partial(near_kernel, stage, region, len(sources)),
            out_shape=pltpu.VMEM(image_shape, F32),
            in_specs=[SMEM_SPEC] + [VMEM_SPEC] * (len(sources) + 2),
            out_specs=VMEM_SPEC,
            scratch_shapes=[stacked] if len(sources) > 1 else [],
            compiler_params=params(),
            cost_estimate=cost(SMALL),
            name="near_stage",
        )(plan, *sources, tiles, total)

    def forward(hop, total):
        arrived[hop], total = lax.optimization_barrier((arrived[hop], total))
        arrived[hop + 1] = exchange(arrived[hop], "row", 1)
        return total

    total = near(0, total)
    for hop in middle:
        total = forward(hop, total)
    total = near(1, total)
    weights, total = lax.optimization_barrier((areas, total))
    basis = pl.pallas_call(
        basis_kernel,
        out_shape=pltpu.VMEM(basis_shape, F32),
        in_specs=[VMEM_SPEC] * 2,
        out_specs=VMEM_SPEC,
        compiler_params=params(),
        cost_estimate=cost(SMALL),
        name="basis_stage",
    )(jnp.transpose(geometry, (1, 0, 2)), weights)
    total = forward(late, total)
    total = near(2, total)

    field, table, powers, crosses = pl.pallas_call(
        functools.partial(field_kernel, 3, region),
        out_shape=(
            pltpu.VMEM(panels.shape, F32),
            pltpu.VMEM(table_shape, F32),
            pltpu.VMEM(power_shape, F32),
            pltpu.VMEM(power_shape, F32),
        ),
        in_specs=[SMEM_SPEC] + [VMEM_SPEC] * 6,
        out_specs=(VMEM_SPEC,) * 4,
        scratch_shapes=[pltpu.VMEM(image_shape, F32)],
        compiler_params=params(),
        cost_estimate=cost(SMALL),
        name="field_stage",
    )(plan, arrived[late + 1], panels, tiles, total, basis, spread)

    tables = [table]
    for distance in range(group_count - 1, 0, -1):
        tables.append(exchange(table, "col", distance))

    gradient = pl.pallas_call(
        functools.partial(gradient_kernel, len(tables)),
        out_shape=jax.ShapeDtypeStruct((block_count, node_count), F32),
        in_specs=[VMEM_SPEC] * (len(tables) + 4),
        out_specs=VMEM_SPEC,
        compiler_params=params(),
        cost_estimate=cost(SMALL),
        name="gradient_stage",
    )(*tables, basis, collect, powers, crosses)
    return (field, gradient)


def solution(mesh):
    in_specs = (
        P(("row", "col"), None, None),
        P(("row", "col"), None, None),
        P(("row", "col")),
        P(("row", "col")),
        P(("row", "col"), None, None),
        P(("row", "col"), None),
        P(("row", "col"), None),
        P(("row", "col")),
    )
    out_specs = (P(("row", "col"), None, None), P(("row", "col"), None))
    return jax.shard_map(shards, mesh=mesh, in_specs=in_specs, out_specs=out_specs, check_vma=False)
```

```python
import functools

import jax
import jax.numpy as jnp
from jax import lax
from jax.experimental import pallas as pl
from jax.experimental.pallas import tpu as pltpu
from jax.sharding import PartitionSpec as P

PD = 4
EPSILON = 1e-05
UNROLL = 16
MOMENTS = 8
SMALL = 1 << 16
STAGE_SHIFT = 16
F32 = jnp.float32
BF16 = jnp.bfloat16
VMEM_LIMIT = 8 << 20
EARLY_LIMIT = 44 << 20

VMEM_SPEC = pl.BlockSpec(memory_space=pltpu.VMEM)
SMEM_SPEC = pl.BlockSpec(memory_space=pltpu.SMEM)
HBM_SPEC = pl.BlockSpec(memory_space=pltpu.HBM)


def cost(size):
    return pl.CostEstimate(flops=0, bytes_accessed=size, transcendentals=0)


def params(limit=VMEM_LIMIT):
    return pltpu.CompilerParams(vmem_limit_bytes=limit)


def parts_of(values, count):
    parts = []
    for _ in range(count - 1):
        part = values.astype(BF16)
        parts.append(part)
        values = values - part.astype(F32)
    parts.append(values.astype(BF16))
    return parts


def dot(left, right, transposed=False):
    axes = (((1,), (1 if transposed else 0,)), ((), ()))
    return lax.dot_general(left, right, axes, preferred_element_type=F32)


def dot_near_exact(left, right, transposed=False):
    rows = left.shape[0]
    left_high, left_low = parts_of(left, 2)
    right_high, right_low = parts_of(right, 2)
    both = dot(jnp.concatenate([left_high, left_low], axis=0), right_high, transposed)
    return both[:rows] + (both[rows:] + dot(left_high, right_low, transposed))


def block_mask(block_count, freq_count):
    shape = (block_count, block_count * freq_count)
    rows = lax.broadcasted_iota(jnp.int32, shape, 0)
    columns = lax.broadcasted_iota(jnp.int32, shape, 1)
    return (columns // freq_count == rows).astype(F32)


def fill_panels(sources, held):
    depth = sources[0].shape[0]
    for index, source in enumerate(sources):
        held[index * depth : (index + 1) * depth] = source[...]


def add_stage(stage, region, plan, held, tiles, total):
    width = plan.shape[0] // 4
    count = plan[3 * width + stage]
    whole = count // UNROLL

    def add_group(base, size):
        images = [
            dot(held[plan[width + base + lane]], tiles[plan[base + lane]])
            for lane in range(size)
        ]
        for lane in range(size):
            target = plan[2 * width + base + lane]
            total[target] += images[lane]

    def body(step, carry):
        add_group(stage * region + step * UNROLL, UNROLL)
        return carry

    lax.fori_loop(0, whole, body, 0)
    left = count - whole * UNROLL
    for size in range(2, UNROLL + 1, 2):

        @pl.when((left > size - 2) & (left <= size))
        def _(size=size):
            add_group(stage * region + whole * UNROLL, size)


def early_kernel(tiles, token):
    token[...] = jnp.zeros_like(token)


def plan_kernel(
    stages, region, freq_count, table, src, dst, owner, slot, token, plan, total, spread, collect
):
    block_count = owner.shape[0]
    width = plan.shape[0] // 4
    me = lax.axis_index("row")

    def place_tile(t, counts):
        source = src[t]
        found = table[lax.div(source, block_count) ^ me]
        stage_here = lax.shift_right_logical(found, STAGE_SHIFT)
        target = jnp.int32(0)
        for stage in range(len(stages)):
            target = jnp.where(stage_here == stage, stage * region + counts[stage], target)
        plan[target] = t
        plan[width + target] = (found & (2**STAGE_SHIFT - 1)) + lax.rem(source, block_count)
        plan[2 * width + target] = dst[t]
        return tuple(
            count + (stage_here == stage).astype(jnp.int32) for stage, count in enumerate(counts)
        )

    counts = lax.fori_loop(0, src.shape[0], place_tile, (jnp.int32(0),) * len(stages), unroll=8)
    for stage in range(len(stages)):
        plan[3 * width + stage] = counts[stage]
        for lane in range(UNROLL):
            position = stage * region + counts[stage] + lane
            plan[position] = 0
            plan[width + position] = 0
            plan[2 * width + position] = block_count
    total[...] = jnp.zeros_like(total)
    shape = (freq_count, spread.shape[1])
    lanes = lax.broadcasted_iota(jnp.int32, shape, 1)
    same = lanes % freq_count == lax.broadcasted_iota(jnp.int32, shape, 0)
    for block in range(block_count):
        particle = owner[block] * PD + slot[block]
        chosen = same & (lanes // freq_count == particle)
        spread[block * freq_count : (block + 1) * freq_count] = jnp.where(
            chosen, 1.0, 0.0
        ).astype(BF16)
    rows = lax.broadcasted_iota(jnp.int32, collect.shape, 0)
    lanes = lax.broadcasted_iota(jnp.int32, collect.shape, 1)
    wanted = lanes % freq_count
    for block in range(block_count):
        particle = owner[block] * PD + slot[block]
        wanted = wanted + jnp.where(lanes // freq_count == block, particle * freq_count, 0)
    collect[...] = jnp.where(rows == wanted, 1.0, 0.0).astype(BF16)


def basis_kernel(place, areas, basis):
    block_count = areas.shape[0]
    nx, ny, nz, px, py, pz = [place[i] for i in range(6)]
    weight = areas[...]
    rows = [nx, ny, nz, py * nz - pz * ny, pz * nx - px * nz, px * ny - py * nx]
    for index, row in enumerate(rows):
        basis[index * block_count : (index + 1) * block_count] = weight * row
    for index in range(len(rows), MOMENTS):
        basis[index * block_count : (index + 1) * block_count] = weight


def near_kernel(stage, region, count, plan, *refs):
    sources = refs[:count]
    tiles, start, total, *held = refs[count:]
    total[...] = start[...]
    if held:
        fill_panels(sources, held[0])
    add_stage(stage, region, plan, held[0] if held else sources[0], tiles, total)


def field_kernel(
    stage, region, plan, source, panels, tiles, start, basis, spread,
    total, table, powers, crosses,
):
    block_count, rows_twice, node_count = panels.shape
    freq_count = rows_twice // 2
    total[...] = start[...]
    add_stage(stage, region, plan, source, tiles, total)
    for block in range(block_count):
        image = total[block]
        incident = panels[block].astype(F32)
        real_in, imag_in = incident[:freq_count], incident[freq_count:]
        real = 0.5 * real_in + (
            image[:freq_count, :node_count] - image[freq_count:, node_count:]
        )
        imag = 0.5 * imag_in + (
            image[:freq_count, node_count:] + image[freq_count:, :node_count]
        )
        span = slice(block * freq_count, (block + 1) * freq_count)
        powers[span] = real * real + imag * imag
        crosses[span] = real_in * real + imag_in * imag
    last = (MOMENTS - 1) * block_count
    first_moments = dot_near_exact(basis[:last], powers[...], True)
    last_moment = dot_near_exact(basis[last:], crosses[...], True)
    mask = block_mask(block_count, freq_count)
    pieces = [
        jnp.sum(mask * first_moments[k * block_count : (k + 1) * block_count], axis=0, keepdims=True)
        for k in range(MOMENTS - 1)
    ]
    pieces.append(jnp.sum(mask * last_moment, axis=0, keepdims=True))
    moments = jnp.concatenate(pieces, axis=0)
    joined = dot(jnp.concatenate(parts_of(moments, 3), axis=0), spread[...])
    table[...] = joined[:MOMENTS] + (joined[MOMENTS : 2 * MOMENTS] + joined[2 * MOMENTS :])


def write_kernel(panels, total, field):
    block_count, rows_twice, node_count = panels.shape
    freq_count = rows_twice // 2
    for block in range(block_count):
        image = total[block]
        incident = panels[block].astype(F32)
        field[block, :freq_count] = 0.5 * incident[:freq_count] + (
            image[:freq_count, :node_count] - image[freq_count:, node_count:]
        )
        field[block, freq_count:] = 0.5 * incident[freq_count:] + (
            image[:freq_count, node_count:] + image[freq_count:, :node_count]
        )


def gradient_kernel(count, *refs):
    tables = refs[:count]
    basis, collect, powers, crosses, gradient = refs[count:]
    block_count = gradient.shape[0]
    freq_count = powers.shape[0] // block_count
    summed = tables[0][...]
    for table in tables[1:]:
        summed = summed + table[...]
    joined = dot(jnp.concatenate(parts_of(summed, 3), axis=0), collect[...])
    totals = joined[:MOMENTS] + (joined[MOMENTS : 2 * MOMENTS] + joined[2 * MOMENTS :])
    mask = block_mask(block_count, freq_count)
    squares = jnp.sum(totals * totals, axis=0, keepdims=True)
    mean = jnp.sum(mask * squares, axis=1, keepdims=True) / (MOMENTS * freq_count)
    scale = lax.rsqrt(mean + EPSILON) / freq_count
    spots = [mask * totals[k : k + 1] for k in range(MOMENTS)]
    first_terms = dot_near_exact(jnp.concatenate(spots[:-1], axis=0), powers[...])
    last_term = dot_near_exact(spots[-1], crosses[...])
    result = basis[(MOMENTS - 1) * block_count :] * last_term
    for k in range(MOMENTS - 1):
        span = slice(k * block_count, (k + 1) * block_count)
        result = result + basis[span] * first_terms[span]
    gradient[...] = result * scale


def exchange(values, axis, hop):
    pairs = [(i, i ^ hop) for i in range(lax.axis_size(axis))]
    return lax.ppermute(values, axis, pairs)


def shards(panels, tiles, tile_dst, tile_src, geometry, areas, block_owner, block_slot):
    block_count, rows_twice, node_count = panels.shape
    freq_count = rows_twice // 2
    tile_count = tiles.shape[0]
    row_count = lax.axis_size("row")
    group_count = lax.axis_size("col")
    particle_count = group_count * PD
    image_shape = (block_count + 1, rows_twice, 2 * node_count)
    basis_shape = (MOMENTS * block_count, node_count)
    spread_shape = (block_count * freq_count, particle_count * freq_count)
    power_shape = (block_count * freq_count, node_count)
    table_shape = (MOMENTS, particle_count * freq_count)
    region = tile_count + UNROLL

    token = pl.pallas_call(
        early_kernel,
        out_shape=pltpu.VMEM((8, 128), F32),
        in_specs=[HBM_SPEC],
        out_specs=VMEM_SPEC,
        compiler_params=params(EARLY_LIMIT),
        cost_estimate=cost(4 * tiles.size),
        name="early_stage",
    )(tiles)

    first, late = row_count // 2, row_count - 2
    middle = [first, *[hop for hop in range(2, row_count, 2) if hop not in (first, late)]]
    stages = ([0], [*middle, 1], [*[hop + 1 for hop in middle], late], [late + 1])
    places = {
        hop: (stage << STAGE_SHIFT) + index * block_count
        for stage, hops in enumerate(stages)
        for index, hop in enumerate(hops)
    }
    table = jnp.array([places[hop] for hop in range(row_count)], jnp.int32)
    width = -(-(len(stages) * region) // 128) * 128

    arrived = {0: panels}
    token, out = lax.optimization_barrier((token, panels))
    for hop in [*middle, late, 1]:
        arrived[hop] = exchange(out, "row", hop)

    plan, total, spread, collect = pl.pallas_call(
        functools.partial(plan_kernel, stages, region, freq_count),
        out_shape=(
            pltpu.SMEM((4 * width,), jnp.int32),
            pltpu.VMEM(image_shape, F32),
            pltpu.VMEM(spread_shape, BF16),
            pltpu.VMEM(spread_shape[::-1], BF16),
        ),
        in_specs=[SMEM_SPEC] * 5 + [VMEM_SPEC],
        out_specs=(SMEM_SPEC,) + (VMEM_SPEC,) * 3,
        compiler_params=params(),
        cost_estimate=cost(4 * tiles.size),
        name="plan_stage",
    )(table, tile_src, tile_dst, block_owner[:, 0], block_slot, token)

    def near(stage, total):
        sources = [arrived[hop] for hop in stages[stage]]
        stacked = pltpu.VMEM((len(sources) * block_count, rows_twice, node_count), BF16)
        return pl.pallas_call(
            functools.partial(near_kernel, stage, region, len(sources)),
            out_shape=pltpu.VMEM(image_shape, F32),
            in_specs=[SMEM_SPEC] + [VMEM_SPEC] * (len(sources) + 2),
            out_specs=VMEM_SPEC,
            scratch_shapes=[stacked] if len(sources) > 1 else [],
            compiler_params=params(),
            cost_estimate=cost(SMALL),
            name="near_stage",
        )(plan, *sources, tiles, total)

    def forward(hop, total):
        arrived[hop], total = lax.optimization_barrier((arrived[hop], total))
        arrived[hop + 1] = exchange(arrived[hop], "row", 1)
        return total

    total = near(0, total)
    for hop in middle:
        total = forward(hop, total)
    total = near(1, total)
    weights, total = lax.optimization_barrier((areas, total))
    basis = pl.pallas_call(
        basis_kernel,
        out_shape=pltpu.VMEM(basis_shape, F32),
        in_specs=[VMEM_SPEC] * 2,
        out_specs=VMEM_SPEC,
        compiler_params=params(),
        cost_estimate=cost(SMALL),
        name="basis_stage",
    )(jnp.transpose(geometry, (1, 0, 2)), weights)
    total = forward(late, total)
    total = near(2, total)

    total, table, powers, crosses = pl.pallas_call(
        functools.partial(field_kernel, 3, region),
        out_shape=(
            pltpu.VMEM(image_shape, F32),
            pltpu.VMEM(table_shape, F32),
            pltpu.VMEM(power_shape, F32),
            pltpu.VMEM(power_shape, F32),
        ),
        in_specs=[SMEM_SPEC] + [VMEM_SPEC] * 6,
        out_specs=(VMEM_SPEC,) * 4,
        compiler_params=params(),
        cost_estimate=cost(SMALL),
        name="field_stage",
    )(plan, arrived[late + 1], panels, tiles, total, basis, spread)

    field = pl.pallas_call(
        write_kernel,
        out_shape=jax.ShapeDtypeStruct(panels.shape, F32),
        in_specs=[VMEM_SPEC] * 2,
        out_specs=VMEM_SPEC,
        compiler_params=params(),
        cost_estimate=cost(SMALL),
        name="write_stage",
    )(panels, total)

    tables = [table]
    for distance in range(group_count - 1, 0, -1):
        tables.append(exchange(table, "col", distance))

    gradient = pl.pallas_call(
        functools.partial(gradient_kernel, len(tables)),
        out_shape=jax.ShapeDtypeStruct((block_count, node_count), F32),
        in_specs=[VMEM_SPEC] * (len(tables) + 4),
        out_specs=VMEM_SPEC,
        compiler_params=params(),
        cost_estimate=cost(SMALL),
        name="gradient_stage",
    )(*tables, basis, collect, powers, crosses)
    return (field, gradient)


def solution(mesh):
    in_specs = (
        P(("row", "col"), None, None),
        P(("row", "col"), None, None),
        P(("row", "col")),
        P(("row", "col")),
        P(("row", "col"), None, None),
        P(("row", "col"), None),
        P(("row", "col"), None),
        P(("row", "col")),
    )
    out_specs = (P(("row", "col"), None, None), P(("row", "col"), None))
    return jax.shard_map(shards, mesh=mesh, in_specs=in_specs, out_specs=out_specs, check_vma=False)
```

```python
import functools

import jax
import jax.numpy as jnp
from jax import lax
from jax.experimental import pallas as pl
from jax.experimental.pallas import tpu as pltpu
from jax.sharding import PartitionSpec as P

PD = 4
EPSILON = 1e-05
UNROLL = 16
MOMENTS = 8
SMALL = 1 << 16
STAGE_SHIFT = 16
F32 = jnp.float32
BF16 = jnp.bfloat16
VMEM_LIMIT = 8 << 20
EARLY_LIMIT = 44 << 20

VMEM_SPEC = pl.BlockSpec(memory_space=pltpu.VMEM)
SMEM_SPEC = pl.BlockSpec(memory_space=pltpu.SMEM)
HBM_SPEC = pl.BlockSpec(memory_space=pltpu.HBM)


def cost(size):
    return pl.CostEstimate(flops=0, bytes_accessed=size, transcendentals=0)


def params(limit=VMEM_LIMIT):
    return pltpu.CompilerParams(vmem_limit_bytes=limit)


def parts_of(values, count):
    parts = []
    for _ in range(count - 1):
        part = values.astype(BF16)
        parts.append(part)
        values = values - part.astype(F32)
    parts.append(values.astype(BF16))
    return parts


def dot(left, right, transposed=False):
    axes = (((1,), (1 if transposed else 0,)), ((), ()))
    return lax.dot_general(left, right, axes, preferred_element_type=F32)


def dot_near_exact(left, right, transposed=False):
    rows = left.shape[0]
    left_high, left_low = parts_of(left, 2)
    right_high, right_low = parts_of(right, 2)
    both = dot(jnp.concatenate([left_high, left_low], axis=0), right_high, transposed)
    return both[:rows] + (both[rows:] + dot(left_high, right_low, transposed))


def block_mask(block_count, freq_count):
    shape = (block_count, block_count * freq_count)
    rows = lax.broadcasted_iota(jnp.int32, shape, 0)
    columns = lax.broadcasted_iota(jnp.int32, shape, 1)
    return (columns // freq_count == rows).astype(F32)


def fill_panels(sources, held):
    depth = sources[0].shape[0]
    for index, source in enumerate(sources):
        held[index * depth : (index + 1) * depth] = source[...]


def add_stage(stage, region, plan, held, tiles, total):
    width = plan.shape[0] // 4
    count = plan[3 * width + stage]
    whole = count // UNROLL

    def add_group(base, size):
        images = [
            dot(held[plan[width + base + lane]], tiles[plan[base + lane]])
            for lane in range(size)
        ]
        for lane in range(size):
            target = plan[2 * width + base + lane]
            total[target] += images[lane]

    def body(step, carry):
        add_group(stage * region + step * UNROLL, UNROLL)
        return carry

    lax.fori_loop(0, whole, body, 0)
    left = count - whole * UNROLL
    for size in range(2, UNROLL + 1, 2):

        @pl.when((left > size - 2) & (left <= size))
        def _(size=size):
            add_group(stage * region + whole * UNROLL, size)


def early_kernel(tiles, token):
    token[...] = jnp.zeros_like(token)


def plan_kernel(
    stages, region, freq_count, table, src, dst, owner, slot, token, plan, total, spread, collect
):
    block_count = owner.shape[0]
    width = plan.shape[0] // 4
    me = lax.axis_index("row")

    def place_tile(t, counts):
        source = src[t]
        found = table[lax.div(source, block_count) ^ me]
        stage_here = lax.shift_right_logical(found, STAGE_SHIFT)
        target = jnp.int32(0)
        for stage in range(len(stages)):
            target = jnp.where(stage_here == stage, stage * region + counts[stage], target)
        plan[target] = t
        plan[width + target] = (found & (2**STAGE_SHIFT - 1)) + lax.rem(source, block_count)
        plan[2 * width + target] = dst[t]
        return tuple(
            count + (stage_here == stage).astype(jnp.int32) for stage, count in enumerate(counts)
        )

    counts = lax.fori_loop(0, src.shape[0], place_tile, (jnp.int32(0),) * len(stages), unroll=8)
    for stage in range(len(stages)):
        plan[3 * width + stage] = counts[stage]
        for lane in range(UNROLL):
            position = stage * region + counts[stage] + lane
            plan[position] = 0
            plan[width + position] = 0
            plan[2 * width + position] = block_count
    total[...] = jnp.zeros_like(total)
    shape = (freq_count, spread.shape[1])
    lanes = lax.broadcasted_iota(jnp.int32, shape, 1)
    same = lanes % freq_count == lax.broadcasted_iota(jnp.int32, shape, 0)
    for block in range(block_count):
        particle = owner[block] * PD + slot[block]
        chosen = same & (lanes // freq_count == particle)
        spread[block * freq_count : (block + 1) * freq_count] = jnp.where(
            chosen, 1.0, 0.0
        ).astype(BF16)
    rows = lax.broadcasted_iota(jnp.int32, collect.shape, 0)
    lanes = lax.broadcasted_iota(jnp.int32, collect.shape, 1)
    wanted = lanes % freq_count
    for block in range(block_count):
        particle = owner[block] * PD + slot[block]
        wanted = wanted + jnp.where(lanes // freq_count == block, particle * freq_count, 0)
    collect[...] = jnp.where(rows == wanted, 1.0, 0.0).astype(BF16)


def basis_kernel(place, areas, basis):
    block_count = areas.shape[0]
    nx, ny, nz, px, py, pz = [place[i] for i in range(6)]
    weight = areas[...]
    rows = [nx, ny, nz, py * nz - pz * ny, pz * nx - px * nz, px * ny - py * nx]
    for index, row in enumerate(rows):
        basis[index * block_count : (index + 1) * block_count] = weight * row
    for index in range(len(rows), MOMENTS):
        basis[index * block_count : (index + 1) * block_count] = weight


def near_kernel(stage, region, count, plan, *refs):
    sources = refs[:count]
    tiles, start, total, *held = refs[count:]
    total[...] = start[...]
    if held:
        fill_panels(sources, held[0])
    add_stage(stage, region, plan, held[0] if held else sources[0], tiles, total)


def field_kernel(
    stage, region, plan, source, panels, tiles, start, basis, spread,
    total, table, powers, crosses,
):
    block_count, rows_twice, node_count = panels.shape
    freq_count = rows_twice // 2
    total[...] = start[...]
    add_stage(stage, region, plan, source, tiles, total)
    for block in range(block_count):
        image = total[block]
        incident = panels[block].astype(F32)
        real_in, imag_in = incident[:freq_count], incident[freq_count:]
        real = 0.5 * real_in + (
            image[:freq_count, :node_count] - image[freq_count:, node_count:]
        )
        imag = 0.5 * imag_in + (
            image[:freq_count, node_count:] + image[freq_count:, :node_count]
        )
        span = slice(block * freq_count, (block + 1) * freq_count)
        powers[span] = real * real + imag * imag
        crosses[span] = real_in * real + imag_in * imag
    last = (MOMENTS - 1) * block_count
    first_moments = dot_near_exact(basis[:last], powers[...], True)
    last_moment = dot_near_exact(basis[last:], crosses[...], True)
    mask = block_mask(block_count, freq_count)
    pieces = [
        jnp.sum(mask * first_moments[k * block_count : (k + 1) * block_count], axis=0, keepdims=True)
        for k in range(MOMENTS - 1)
    ]
    pieces.append(jnp.sum(mask * last_moment, axis=0, keepdims=True))
    moments = jnp.concatenate(pieces, axis=0)
    joined = dot(jnp.concatenate(parts_of(moments, 3), axis=0), spread[...])
    table[...] = joined[:MOMENTS] + (joined[MOMENTS : 2 * MOMENTS] + joined[2 * MOMENTS :])


def write_kernel(panels, total, field):
    block_count, rows_twice, node_count = panels.shape
    freq_count = rows_twice // 2
    for block in range(block_count):
        image = total[block]
        incident = panels[block].astype(F32)
        field[block, :freq_count] = 0.5 * incident[:freq_count] + (
            image[:freq_count, :node_count] - image[freq_count:, node_count:]
        )
        field[block, freq_count:] = 0.5 * incident[freq_count:] + (
            image[:freq_count, node_count:] + image[freq_count:, :node_count]
        )


def gradient_kernel(count, *refs):
    tables = refs[:count]
    basis, collect, powers, crosses, gradient = refs[count:]
    block_count = gradient.shape[0]
    freq_count = powers.shape[0] // block_count
    summed = tables[0][...]
    for table in tables[1:]:
        summed = summed + table[...]
    joined = dot(jnp.concatenate(parts_of(summed, 3), axis=0), collect[...])
    totals = joined[:MOMENTS] + (joined[MOMENTS : 2 * MOMENTS] + joined[2 * MOMENTS :])
    mask = block_mask(block_count, freq_count)
    squares = jnp.sum(totals * totals, axis=0, keepdims=True)
    mean = jnp.sum(mask * squares, axis=1, keepdims=True) / (MOMENTS * freq_count)
    scale = lax.rsqrt(mean + EPSILON) / freq_count
    spots = [mask * totals[k : k + 1] for k in range(MOMENTS)]
    first_terms = dot_near_exact(jnp.concatenate(spots[:-1], axis=0), powers[...])
    last_term = dot_near_exact(spots[-1], crosses[...])
    result = basis[(MOMENTS - 1) * block_count :] * last_term
    for k in range(MOMENTS - 1):
        span = slice(k * block_count, (k + 1) * block_count)
        result = result + basis[span] * first_terms[span]
    gradient[...] = result * scale


def exchange(values, axis, hop):
    pairs = [(i, i ^ hop) for i in range(lax.axis_size(axis))]
    return lax.ppermute(values, axis, pairs)


def shards(panels, tiles, tile_dst, tile_src, geometry, areas, block_owner, block_slot):
    block_count, rows_twice, node_count = panels.shape
    freq_count = rows_twice // 2
    tile_count = tiles.shape[0]
    row_count = lax.axis_size("row")
    group_count = lax.axis_size("col")
    particle_count = group_count * PD
    image_shape = (block_count + 1, rows_twice, 2 * node_count)
    basis_shape = (MOMENTS * block_count, node_count)
    spread_shape = (block_count * freq_count, particle_count * freq_count)
    power_shape = (block_count * freq_count, node_count)
    table_shape = (MOMENTS, particle_count * freq_count)
    region = tile_count + UNROLL

    token = pl.pallas_call(
        early_kernel,
        out_shape=pltpu.VMEM((8, 128), F32),
        in_specs=[HBM_SPEC],
        out_specs=VMEM_SPEC,
        compiler_params=params(EARLY_LIMIT),
        cost_estimate=cost(4 * tiles.size),
        name="early_stage",
    )(tiles)

    first, late = row_count // 2, row_count - 2
    middle = [first, *[hop for hop in range(2, row_count, 2) if hop not in (first, late)]]
    stages = ([0], [*middle, 1], [*[hop + 1 for hop in middle], late], [late + 1])
    places = {
        hop: (stage << STAGE_SHIFT) + index * block_count
        for stage, hops in enumerate(stages)
        for index, hop in enumerate(hops)
    }
    table = jnp.array([places[hop] for hop in range(row_count)], jnp.int32)
    width = -(-(len(stages) * region) // 128) * 128

    arrived = {0: panels}
    token, out = lax.optimization_barrier((token, panels))
    for hop in [*middle, late, 1]:
        arrived[hop] = exchange(out, "row", hop)

    plan, total, spread, collect = pl.pallas_call(
        functools.partial(plan_kernel, stages, region, freq_count),
        out_shape=(
            pltpu.SMEM((4 * width,), jnp.int32),
            pltpu.VMEM(image_shape, F32),
            pltpu.VMEM(spread_shape, BF16),
            pltpu.VMEM(spread_shape[::-1], BF16),
        ),
        in_specs=[SMEM_SPEC] * 5 + [VMEM_SPEC],
        out_specs=(SMEM_SPEC,) + (VMEM_SPEC,) * 3,
        compiler_params=params(),
        cost_estimate=cost(4 * tiles.size),
        name="plan_stage",
    )(table, tile_src, tile_dst, block_owner[:, 0], block_slot, token)

    def near(stage, total):
        sources = [arrived[hop] for hop in stages[stage]]
        stacked = pltpu.VMEM((len(sources) * block_count, rows_twice, node_count), BF16)
        return pl.pallas_call(
            functools.partial(near_kernel, stage, region, len(sources)),
            out_shape=pltpu.VMEM(image_shape, F32),
            in_specs=[SMEM_SPEC] + [VMEM_SPEC] * (len(sources) + 2),
            out_specs=VMEM_SPEC,
            scratch_shapes=[stacked] if len(sources) > 1 else [],
            compiler_params=params(),
            cost_estimate=cost(SMALL),
            name="near_stage",
        )(plan, *sources, tiles, total)

    def forward(hop, total):
        arrived[hop], total = lax.optimization_barrier((arrived[hop], total))
        arrived[hop + 1] = exchange(arrived[hop], "row", 1)
        return total

    total = near(0, total)
    for hop in middle:
        total = forward(hop, total)
    total = near(1, total)
    weights, total = lax.optimization_barrier((areas, total))
    basis = pl.pallas_call(
        basis_kernel,
        out_shape=pltpu.VMEM(basis_shape, F32),
        in_specs=[VMEM_SPEC] * 2,
        out_specs=VMEM_SPEC,
        compiler_params=params(),
        cost_estimate=cost(SMALL),
        name="basis_stage",
    )(jnp.transpose(geometry, (1, 0, 2)), weights)
    total = forward(late, total)
    total = near(2, total)

    total, table, powers, crosses = pl.pallas_call(
        functools.partial(field_kernel, 3, region),
        out_shape=(
            pltpu.VMEM(image_shape, F32),
            pltpu.VMEM(table_shape, F32),
            pltpu.VMEM(power_shape, F32),
            pltpu.VMEM(power_shape, F32),
        ),
        in_specs=[SMEM_SPEC] + [VMEM_SPEC] * 6,
        out_specs=(VMEM_SPEC,) * 4,
        compiler_params=params(),
        cost_estimate=cost(SMALL),
        name="field_stage",
    )(plan, arrived[late + 1], panels, tiles, total, basis, spread)

    field = pl.pallas_call(
        write_kernel,
        out_shape=jax.ShapeDtypeStruct(panels.shape, F32),
        in_specs=[VMEM_SPEC] * 2,
        out_specs=VMEM_SPEC,
        compiler_params=params(),
        cost_estimate=cost(SMALL),
        name="write_stage",
    )(panels, total)

    tables = [table]
    distances = list(range(1, group_count))
    for distance in distances[-1:] + distances[:-1]:
        tables.append(exchange(table, "col", distance))

    gradient = pl.pallas_call(
        functools.partial(gradient_kernel, len(tables)),
        out_shape=jax.ShapeDtypeStruct((block_count, node_count), F32),
        in_specs=[VMEM_SPEC] * (len(tables) + 4),
        out_specs=VMEM_SPEC,
        compiler_params=params(),
        cost_estimate=cost(SMALL),
        name="gradient_stage",
    )(*tables, basis, collect, powers, crosses)
    return (field, gradient)


def solution(mesh):
    in_specs = (
        P(("row", "col"), None, None),
        P(("row", "col"), None, None),
        P(("row", "col")),
        P(("row", "col")),
        P(("row", "col"), None, None),
        P(("row", "col"), None),
        P(("row", "col"), None),
        P(("row", "col")),
    )
    out_specs = (P(("row", "col"), None, None), P(("row", "col"), None))
    return jax.shard_map(shards, mesh=mesh, in_specs=in_specs, out_specs=out_specs, check_vma=False)
```
